512 devices in a mesh: wide: 128 (over z, x, y_lo), narrow: 4 (over y_hi, core).
Axes of the slice: x: 4, y: 4 (y_hi: 2, y_lo: 2; y = y_hi * 2 + y_lo), z: 16, core: 2. Of those that a mesh axis runs over, the one named last changes fastest.
Arguments:
- rhs: float32 [64, 1024, 1024], P(None, 'wide', 'narrow'), may hold values from -6 to 6
- areas: float32 [1024, 1024], P('wide', 'narrow'), may hold values from 0.5 to 2
- stiffness: float32 [64], replicated, may hold values from 1e-07 to 1
Outputs:
- pressure: float32 [64, 1024, 1024], P(None, 'wide', 'narrow')
- residual: float32 [64, 1024, 1024], P(None, 'wide', 'narrow')
The draws below stay inside these ranges and needn't reach their ends.
All inputs are finite; a program needn't handle non-finite values.
Results may differ from the reference program's by a relative error of at most 0.0003.
Values sent between devices are 32-bit elements; how exact they have to be, the bound alone decides.
No kernel may reach another device: no remote copies, remote signals or barrier semaphores. Data moves between devices by JAX's collectives and lax.ppermute only.
A program may use at most 64 MiB of HBM per device.

```python
import math
import jax
import jax.numpy as jnp
from jax import lax

K = 64
NX = 1024
NY = 1024


def shard_levels(key, shape, split, least, high):
    def one(axis_at, shards_of):
        draws = jax.random.uniform(jax.random.fold_in(jax.random.fold_in(key, 6), axis_at), (shards_of,), jnp.float32, least / len(split), high / len(split))
        return jnp.repeat(jnp.exp(draws), shape[axis_at] // shards_of).reshape((-1,) + (1,) * (len(shape) - axis_at - 1))

    factor_of = one(*split[0])
    for cut in split[1:]:
        factor_of = factor_of * one(*cut)
    return factor_of


def centred(stream_key, shape, deviation, most, shards=(), kind=jnp.bfloat16):
    values = deviation * jax.random.normal(stream_key, shape, jnp.float32)
    if shards:
        values = values * shard_levels(stream_key, shape, shards, -0.22, 0.18)
    return jnp.clip(values, -most, most).astype(kind)


def setup_inputs(seed: int = 0) -> dict:
    seeds = jax.random.split(jax.random.key(seed), 4)
    return {
        "rhs": centred(seeds[0], (K, NX, NY), 1.0, 6.0, ((1, 128), (2, 4)), jnp.float32),
        "areas": jnp.clip(jnp.exp(math.log(2.0) - 1.3862944 * jax.random.uniform(seeds[1], (NX, NY), jnp.float32) ** shard_levels(seeds[1], (NX, NY), ((0, 128), (1, 4)), -0.2, 0.2)), 0.5, 2.0),
        "stiffness": jnp.clip(jnp.exp(jax.random.uniform(seeds[2], (K,), jnp.float32, math.log(1.0000000116860974e-07), math.log(1.0))), 1.0000000116860974e-07, 1.0),
    }


coupling = 2.0
relaxation = 0.4

def column_inverse(stiffness):
    levels = stiffness.shape[0]
    identity_k = jnp.eye(levels, dtype=stiffness.dtype)
    neighbours = jnp.eye(levels, k=1, dtype=stiffness.dtype) + jnp.eye(levels, k=-1, dtype=stiffness.dtype)
    matrix = jnp.diag(stiffness + 2.0 * coupling + 4.0) - coupling * neighbours
    lower = jnp.linalg.cholesky(matrix)
    lower_inv = lax.linalg.triangular_solve(lower, identity_k, left_side=True, lower=True)
    return jnp.dot(lower_inv.T, lower_inv, precision=lax.Precision.HIGHEST)

def apply_columns(inverse, field):
    return jnp.einsum('kl,lxy->kxy', inverse, field, precision=lax.Precision.HIGHEST)

def vertical(field, stiffness):
    empty = jnp.zeros_like(field[:1])
    above = jnp.concatenate([field[1:], empty], axis=0)
    below = jnp.concatenate([empty, field[:-1]], axis=0)
    return stiffness[:, None, None] * field + coupling * (2.0 * field - above - below)

def operate(padded, coef, stiffness):
    center = padded[:, 1:-1, 1:-1]
    beside = padded[:, 2:, 1:-1] + padded[:, :-2, 1:-1] + padded[:, 1:-1, 2:] + padded[:, 1:-1, :-2]
    return vertical(center, stiffness) + coef[None] * (4.0 * center - beside)

def coarsen(field):
    return 0.25 * (field[..., 0::2, 0::2] + field[..., 1::2, 0::2] + field[..., 0::2, 1::2] + field[..., 1::2, 1::2])

def line_factors(stiffness):
    gain_in = jnp.sqrt(stiffness + 0.25 * stiffness * stiffness) - 0.5 * stiffness
    return (gain_in, 1.0 - gain_in)

def pad_zero(field):
    return jnp.pad(field, ((0, 0), (1, 1), (1, 1)))

def reference(rhs, areas, stiffness):
    inverse = column_inverse(stiffness)

    def residual_of(field):
        return rhs - operate(pad_zero(field), areas, stiffness)
    field = relaxation * apply_columns(inverse, rhs)
    field = field + relaxation * apply_columns(inverse, residual_of(field))
    coarse_rhs = coarsen(residual_of(field))
    coarse_coef = 0.25 * coarsen(areas)
    gain_in, retain = line_factors(stiffness)

    def advance(carry, column):
        fresh = gain_in[:, None] * column + retain[:, None] * carry
        return (fresh, fresh)
    columns = jnp.moveaxis(coarse_rhs, 1, 0)
    empty = jnp.zeros_like(columns[0])
    _, forward = lax.scan(advance, empty, columns)
    _, backward = lax.scan(advance, empty, forward, reverse=True)
    line_corr = jnp.moveaxis(backward, 0, 1)
    coarse_corr = line_corr + relaxation * apply_columns(inverse, coarse_rhs - operate(pad_zero(line_corr), coarse_coef, stiffness))
    field = field + jnp.repeat(jnp.repeat(coarse_corr, 2, axis=1), 2, axis=2)
    field = field + relaxation * apply_columns(inverse, residual_of(field))
    field = field + relaxation * apply_columns(inverse, residual_of(field))
    return (field, residual_of(field))
```

```python
import functools

import jax
import jax.numpy as jnp
from jax import lax
from jax.experimental import pallas as pl
from jax.experimental.pallas import tpu as pltpu
from jax.sharding import PartitionSpec as P

K = 64
KA = 72
HX = 6
HY = 8
NR = 8 + 2 * HX
YP = -(-HY * NR // 128) * 128
LX = 384
PLANE = 8
f32, bf16 = jnp.float32, jnp.bfloat16
LIMIT = 32 * 1024 * 1024


def call(kernel, outs, scratch=(), specs=None):
    vmem = pl.BlockSpec(memory_space=pltpu.VMEM)
    return pl.pallas_call(
        kernel,
        out_shape=[jax.ShapeDtypeStruct(s, d) for s, d in outs],
        in_specs=specs,
        out_specs=[vmem] * len(outs),
        scratch_shapes=list(scratch),
        compiler_params=pltpu.CompilerParams(vmem_limit_bytes=LIMIT),
    )


def on_vmem(n):
    return [pl.BlockSpec(memory_space=pltpu.VMEM)] * n


def lanes(shape):
    return lax.broadcasted_iota(jnp.int32, shape, len(shape) - 1)


def wide3(table):
    return jnp.concatenate([table] * (LX // 128), axis=1)


def apply3(cat, x):
    high = x.astype(bf16)
    low = (x - high.astype(f32)).astype(bf16)
    return jnp.dot(cat, jnp.concatenate([high, high, low], axis=0), preferred_element_type=f32)


def split3(matrix):
    high = matrix.astype(bf16)
    low = (matrix - high.astype(f32)).astype(bf16)
    return jnp.concatenate([high, low, high], axis=1)


def own_row(rhs_ref, areas_ref, x):
    return (
        jnp.concatenate([rhs_ref[pl.ds(8 * t + x, K, stride=16), :] for t in range(2)], axis=1),
        jnp.broadcast_to(areas_ref[pl.ds(x, 1), :], (KA - K, 256)),
    )


def pack_x(rhs_ref, areas_ref, up_ref, down_ref):
    for x in range(8):
        field, area = own_row(rhs_ref, areas_ref, x)
        if x < HX:
            down_ref[x, :K, :] = field
            down_ref[x, K:, :] = area
        if x >= 8 - HX:
            up_ref[x - 8 + HX, :K, :] = field
            up_ref[x - 8 + HX, K:, :] = area


def tables(stiff_ref, smooth_ref, vert_ref, retain_ref, weight_ref, lead, trail):
    scale = 7.5
    row = lax.broadcasted_iota(jnp.int32, (K, 128), 0)
    col = lax.broadcasted_iota(jnp.int32, (K, 128), 1)
    lane = lanes((1, 128))
    one = jnp.ones((1, 128), f32)
    zero = jnp.zeros((1, 128), f32)
    before, now, lead_row = zero, one, zero
    after, later, trail_row = zero, one, zero
    for k in range(K):
        lead[pl.ds(k, 1), :] = now
        lead_row = jnp.where(lane == k, now, lead_row)
        now, before = (stiff_ref[k] + 8.0) * (1.0 / scale) * now - (4.0 / scale**2) * before, now
        at = K - 1 - k
        trail[pl.ds(at, 1), :] = later
        trail_row = jnp.where(lane == at, later, trail_row)
        later, after = (stiff_ref[at] + 8.0) * (1.0 / scale) * later - (4.0 / scale**2) * after, later
    gap = jnp.abs(row - col)
    decay = jnp.ones((K, 128), f32)
    for b in range(6):
        decay = decay * jnp.where((gap >> b) & 1 == 1, (2.0 / scale) ** (1 << b), 1.0)
    upper = lead[...] * trail_row
    lower = lead_row * trail[...]
    inverse = decay * jnp.where(row <= col, upper, lower) / (scale * now)
    smooth_ref[...] = split3((0.4 * inverse)[:, :K])
    stiff_row = zero
    for k in range(K):
        stiff_row = jnp.where(lane == k, stiff_ref[k], stiff_row)
    diagonal = jnp.where(row == col, stiff_row, 0.0)
    stiff = jnp.broadcast_to(jnp.sum(diagonal, axis=1, keepdims=True), (K, 128))
    vert = jnp.where(row == col, stiff + 4.0, jnp.where(gap == 1, -2.0, 0.0))
    vert_ref[...] = split3(vert[:, :K])
    keep = jnp.sqrt(stiff + 0.25 * stiff * stiff) - 0.5 * stiff
    retain_ref[...] = 1.0 - keep
    weight_ref[...] = keep / (2.0 - keep)


def ext_row(rhs_ref, areas_ref, left_ref, right_ref, r):
    if r < HX:
        return left_ref[r]
    if r >= HX + 8:
        return right_ref[r - HX - 8]
    return jnp.concatenate(own_row(rhs_ref, areas_ref, r - HX), axis=0)


def pack_y(rhs_ref, areas_ref, left_ref, right_ref, low_ref, high_ref):
    lane = lanes((KA, 128))
    low = [jnp.zeros((KA, 128), f32)] * (YP // 128)
    high = list(low)
    for r in range(NR):
        row = ext_row(rhs_ref, areas_ref, left_ref, right_ref, r)
        t, o = divmod(HY * r, 128)
        here = (lane >= o) & (lane < o + HY)
        low[t] = jnp.where(here, pltpu.roll(row[:, :128], o, 1), low[t])
        high[t] = jnp.where(here, pltpu.roll(row[:, 128:], (o + HY) % 128, 1), high[t])
    low_ref[...] = jnp.concatenate(low, axis=1)
    high_ref[...] = jnp.concatenate(high, axis=1)


def smooth_term(u, rhs, area, above, below, step):
    beside = above + below + pltpu.roll(u, step, 1) + pltpu.roll(u, LX - step, 1)
    return rhs - area * (4.0 * u - beside)


def pair_sum(v):
    even = lanes(v.shape) % 2 == 0
    return v + jnp.where(even, pltpu.roll(v, LX - 1, 1), pltpu.roll(v, 1, 1))


def before_scan(
    rhs_ref, areas_ref, left_ref, right_ref, from_left, from_right, smooth_ref, vert_ref, retain_ref,
    sent_ref, ext_ref, u2_ref, coarse_ref, u1, fine,
):
    lane = lanes((KA, 128))
    for r in range(NR):
        row = ext_row(rhs_ref, areas_ref, left_ref, right_ref, r)
        t, o = divmod(HY * r, 128)
        right = pltpu.roll(from_right[:, 128 * t : 128 * t + 128], (128 - o) % 128, 1)
        left = pltpu.roll(from_left[:, 128 * t : 128 * t + 128], (128 - HY - o) % 128, 1)
        beyond = jnp.where(lane < HY, right, jnp.where(lane >= 128 - HY, left, 0.0))
        ext_ref[r, :, :256] = row
        ext_ref[r, :, 256:] = beyond

    smooth = smooth_ref[...]

    def first(r, _):
        u1[r] = apply3(smooth, ext_ref[r, :K, :])
        return 0

    lax.fori_loop(0, NR, first, 0, unroll=2)

    def second(r, _):
        u = u1[r]
        term = smooth_term(u, ext_ref[r, :K, :] + 4.0 * u, ext_ref[r, K : K + 1, :], u1[r - 1], u1[r + 1], 1)
        fine[r] = 0.6 * u + apply3(smooth, term)
        return 0

    lax.fori_loop(1, NR - 1, second, 0, unroll=2)
    vert = vert_ref[...]

    def third(j, _):
        r = 2 * j + HX - 4
        total, field = 0.0, 0.0
        for at in (r, r + 1):
            u = fine[at]
            total += smooth_term(u, ext_ref[at, :K, :], ext_ref[at, K : K + 1, :], fine[at - 1], fine[at + 1], 1)
            field += u
        coarse_ref[j] = 0.25 * (pair_sum(total) - apply3(vert, pair_sum(field)))
        return 0

    lax.fori_loop(0, 8, third, 0)
    for r in range(14):
        u2_ref[r] = fine[r + HX - 3]
    retain = wide3(retain_ref[...])
    ahead = coarse_ref[2]
    back = coarse_ref[5]
    for j in range(1, 4):
        ahead = retain * ahead + coarse_ref[2 + j]
        back = retain * back + coarse_ref[5 - j]
    fine_lane = lax.broadcasted_iota(jnp.int32, (LX, 256), 0)
    coarse_lane = lax.broadcasted_iota(jnp.int32, (LX, 256), 1)
    pick = jnp.where(fine_lane == 2 * coarse_lane, 1.0, 0.0)
    both = jnp.dot(
        jnp.concatenate([ahead, back], axis=0), pick, precision=lax.Precision.HIGHEST, preferred_element_type=f32
    )
    sent_ref[:, :128] = both[:K, :128]
    sent_ref[:, 128:256] = both[K:, :128]
    sent_ref[:, 256:] = both[:K, 128:] + pltpu.roll(both[K:, 128:], 64, 1)


def power(x, n):
    out = None
    while n:
        if n & 1:
            out = x if out is None else out * x
        x = x * x
        n >>= 1
    return out


def my_retain(retain_ref):
    at = lax.rem(lax.axis_index("wide"), PLANE)
    return retain_ref[pl.ds(pl.multiple_of(at * 8, 8), 8), :]


def plane_ends(blocks, retain):
    four = power(retain, 4)
    ends = []
    for order, part in ((range(PLANE), 0), (reversed(range(PLANE)), 1)):
        main, tail = 0.0, 0.0
        for m in order:
            main = four * main + blocks[m, :, 128 * part : 128 * part + 128]
            tail = four * tail + blocks[m, :, 256:]
        ends += [main, tail if part == 0 else pltpu.roll(tail, 64, 1)]
    return ends


def across_out(planes, blocks_ref, retain_ref, out_ref):
    retain = my_retain(retain_ref)
    here = lax.div(lax.axis_index("wide"), PLANE)
    ahead, ahead_tail, back, back_tail = plane_ends(blocks_ref, retain)
    reflect = power(retain, 33)
    step = power(retain, 64)
    for q in range(planes):
        reflect = jnp.where(q > here, reflect * step, reflect)
    back = back - reflect * ahead
    back_tail = back_tail - reflect * ahead_tail
    for q in range(planes):
        out_ref[q, :, :128] = jnp.where(q > here, ahead, back)
        out_ref[q, :, 128:] = jnp.where(q > here, ahead_tail, back_tail)


def across_in(planes, blocks_ref, others_ref, retain_ref, out_ref):
    retain = my_retain(retain_ref)
    here = lax.div(lax.axis_index("wide"), PLANE)
    ahead, ahead_tail, _, _ = plane_ends(blocks_ref, retain)
    four, plane = power(retain, 4), power(retain, 32)
    reflect, step = retain, power(retain, 64)
    enter, leave = [0.0, 0.0], [0.0, 0.0]
    for q in range(planes):
        reflect = jnp.where(q > here, reflect * step, reflect)
        back = planes - 1 - q
        for part in range(2):
            at = slice(128 * part, 128 * part + 128)
            enter[part] = jnp.where(q < here, plane * enter[part] + others_ref[q, :, at], enter[part])
            leave[part] = jnp.where(back > here, plane * leave[part] + others_ref[back, :, at], leave[part])
    leave[0] = leave[0] - reflect * (ahead + plane * enter[0])
    leave[1] = leave[1] - reflect * (ahead_tail + plane * enter[1])
    left = lanes((8, 128)) < 64
    leave[1] = pltpu.roll(leave[1], 64, 1)
    tails = []
    for m in range(PLANE):
        out_ref[m, :, :128] = enter[0]
        tails.append(enter[1])
        enter[0] = four * enter[0] + blocks_ref[m, :, :128]
        enter[1] = four * enter[1] + blocks_ref[m, :, 256:]
    for m in reversed(range(PLANE)):
        out_ref[m, :, 128:256] = leave[0]
        out_ref[m, :, 256:] = jnp.where(left, tails[m], leave[1])
        leave[0] = four * leave[0] + blocks_ref[m, :, 128:256]
        leave[1] = four * leave[1] + blocks_ref[m, :, 256:]


def after_scan(
    got_ref, ext_ref, u2_ref, coarse_ref, smooth_ref, vert_ref, retain_ref, weight_ref,
    pressure_ref, residual_ref, line, corr, ua, ub,
):
    retain, weight = wide3(retain_ref[...]), wide3(weight_ref[...])
    inv_retain = 1.0 / retain
    coarse_lane = lax.broadcasted_iota(jnp.int32, (256, LX), 0)
    fine_lane = lax.broadcasted_iota(jnp.int32, (256, LX), 1)
    spread = jnp.where(fine_lane // 2 == coarse_lane, 1.0, 0.0)
    keep_left = lanes((K, 128)) < 64
    tail = got_ref[:, 256:]
    both = jnp.concatenate(
        [
            jnp.concatenate([got_ref[:, :128], jnp.where(keep_left, tail, 0.0)], axis=1),
            jnp.concatenate([got_ref[:, 128:256], jnp.where(keep_left, pltpu.roll(tail, 64, 1), 0.0)], axis=1),
        ],
        axis=0,
    )
    both = jnp.dot(both, spread, precision=lax.Precision.HIGHEST, preferred_element_type=f32)

    def coef(j):
        r = 2 * j + HX - 4
        return 0.0625 * pair_sum(ext_ref[r, K : K + 1, :] + ext_ref[r + 1, K : K + 1, :])

    enter, leave = both[:K], both[K:]
    reach = leave
    for j in (4, 5):
        reach = (reach - coarse_ref[j + 2]) * inv_retain
        line[j + 1 + 3] = reach
    reach = leave
    line[4 + 3] = reach
    for j in (3, 2, 1, 0, -1, -2):
        reach = coarse_ref[j + 2] + retain * reach
        line[j + 3] = reach
    ahead = (enter - coarse_ref[1]) * inv_retain
    ahead = (ahead - coarse_ref[0]) * inv_retain
    line[0] = jnp.where(coef(0) > 0.0, weight * (ahead + retain * line[1]), 0.0)
    for j in range(-2, 7):
        inside = coef(min(max(j + 2, 0), 7)) > 0.0
        start = retain * ahead
        line[j + 3] = jnp.where(inside, weight * (start + line[j + 3]), 0.0)
        if j < 6:
            ahead = enter if j == -1 else coarse_ref[j + 2] + start

    smooth = smooth_ref[...]

    def coarse(j, _):
        v = line[j + 1]
        area = coef(j)
        term = smooth_term(v, coarse_ref[j] + 4.0 * v, area, line[j], line[j + 2], 2)
        corr[j] = 0.6 * v + apply3(smooth, term)
        return 0

    lax.fori_loop(0, 8, coarse, 0)
    for i in range(14):
        ua[i] = u2_ref[i] + corr[(i - 3) // 2 + 2]

    def smoothing(source, target, i):
        u = source[i]
        r = i + HX - 3
        term = smooth_term(u, ext_ref[r, :K, :] + 4.0 * u, ext_ref[r, K : K + 1, :], source[i - 1], source[i + 1], 1)
        target[i] = 0.6 * u + apply3(smooth, term)
        return 0

    lax.fori_loop(1, 13, lambda i, _: smoothing(ua, ub, i), 0, unroll=2)
    lax.fori_loop(2, 12, lambda i, _: smoothing(ub, ua, i), 0, unroll=2)
    vert = vert_ref[...]
    for x in range(8):
        i = x + 3
        u = ua[i]
        r = x + HX
        term = smooth_term(u, ext_ref[r, :K, :], ext_ref[r, K : K + 1, :], ua[i - 1], ua[i + 1], 1)
        rest = term[:, :256] - apply3(vert, u[:, :256])
        for t in range(2):
            here = pl.ds(8 * t + x, K, stride=16)
            pressure_ref[here, :] = u[:, 128 * t : 128 * t + 128]
            residual_ref[here, :] = rest[:, 128 * t : 128 * t + 128]


def local(rhs, areas, stiffness):
    wide, narrow = lax.axis_size("wide"), lax.axis_size("narrow")
    planes = wide // PLANE
    rhs = rhs.reshape(K, 8, 2, 128).transpose(0, 2, 1, 3).reshape(K * 16, 128)
    up, down = call(pack_x, [((HX, KA, 256), f32)] * 2, specs=on_vmem(2))(rhs, areas)

    def shift(array, axis, count, by):
        pairs = [(i, i + by) for i in range(count) if 0 <= i + by < count]
        return lax.ppermute(array, axis, pairs)

    left = shift(up, "wide", wide, 1)
    right = shift(down, "wide", wide, -1)
    smooth, vert, retain, weight = call(
        tables,
        [((K, 192), bf16)] * 2 + [((K, 128), f32)] * 2,
        [pltpu.VMEM((K, 128), f32)] * 2,
        [pl.BlockSpec(memory_space=pltpu.SMEM)],
    )(stiffness)
    low, high = call(pack_y, [((KA, YP), f32)] * 2, specs=on_vmem(4))(rhs, areas, left, right)
    from_left = shift(high, "narrow", narrow, 1)
    from_right = shift(low, "narrow", narrow, -1)
    sent, ext, u2, coarse = call(
        before_scan,
        [((K, LX), f32), ((NR, KA, LX), f32), ((14, K, LX), f32), ((8, K, LX), f32)],
        [pltpu.VMEM((NR, K, LX), f32)] * 2,
        on_vmem(9),
    )(rhs, areas, left, right, from_left, from_right, smooth, vert, retain)
    in_plane = [[p * PLANE + m for m in range(PLANE)] for p in range(planes)]
    over_planes = [[p * PLANE + m for p in range(planes)] for m in range(PLANE)]

    def exchange(array, groups):
        return lax.all_to_all(array, "wide", 0, 0, tiled=True, axis_index_groups=groups)

    blocks = exchange(sent.reshape(PLANE, 8, LX), in_plane)
    (out,) = call(functools.partial(across_out, planes), [((planes, 8, 256), f32)], specs=on_vmem(2))(blocks, retain)
    others = exchange(out, over_planes)
    (back,) = call(functools.partial(across_in, planes), [((PLANE, 8, LX), f32)], specs=on_vmem(3))(
        blocks, others, retain
    )
    got = exchange(back, in_plane).reshape(K, LX)
    pressure, residual = call(
        after_scan,
        [((K * 16, 128), f32)] * 2,
        [pltpu.VMEM((10, K, LX), f32), pltpu.VMEM((8, K, LX), f32)] + [pltpu.VMEM((14, K, LX), f32)] * 2,
        on_vmem(8),
    )(got, ext, u2, coarse, smooth, vert, retain, weight)
    return tuple(
        out.reshape(K, 2, 8, 128).transpose(0, 2, 1, 3).reshape(K, 8, 256) for out in (pressure, residual)
    )


def solution(mesh):
    placed = (P(None, "wide", "narrow"), P("wide", "narrow"), P())
    return jax.shard_map(
        local,
        mesh=mesh,
        in_specs=placed,
        out_specs=(P(None, "wide", "narrow"), P(None, "wide", "narrow")),
        check_vma=False,
    )
```

```python
import functools

import jax
import jax.numpy as jnp
from jax import lax
from jax.experimental import pallas as pl
from jax.experimental.pallas import tpu as pltpu
from jax.sharding import PartitionSpec as P

K = 64
KA = 72
HX = 2
HY = 8
NR = 8 + 2 * HX
LX = 384
PLANE = 8
f32, bf16 = jnp.float32, jnp.bfloat16
DEEP_LATE = True
K2_OUTS = [((K, LX), f32), ((NR, KA, 128), f32), ((8, K, LX), f32), ((4, K, LX), f32)]
K2_SCRATCH = [pltpu.VMEM((NR, K, 128), f32), pltpu.VMEM((NR, K, LX), f32)]
K4_SCRATCH = [pltpu.VMEM(s, f32) for s in ((8, K, LX), (10, K, LX), (8, K, LX), (14, K, LX), (14, K, LX))]
LIMIT = 16 * 1024 * 1024


def call(kernel, outs, scratch=(), specs=None):
    vmem = pl.BlockSpec(memory_space=pltpu.VMEM)
    return pl.pallas_call(
        kernel,
        out_shape=[jax.ShapeDtypeStruct(s, d) for s, d in outs],
        in_specs=specs,
        out_specs=[vmem] * len(outs),
        scratch_shapes=list(scratch),
        compiler_params=pltpu.CompilerParams(vmem_limit_bytes=LIMIT),
    )


def on_vmem(n):
    return [pl.BlockSpec(memory_space=pltpu.VMEM)] * n


def lanes(shape):
    return lax.broadcasted_iota(jnp.int32, shape, len(shape) - 1)


def wide3(table):
    return jnp.concatenate([table] * (LX // 128), axis=1)


def apply3(cat, x):
    high = x.astype(bf16)
    low = (x - high.astype(f32)).astype(bf16)
    return jnp.dot(cat, jnp.concatenate([high, high, low], axis=0), preferred_element_type=f32)


def select(x, picks):
    high = x.astype(bf16)
    rest = x - high.astype(f32)
    middle = rest.astype(bf16)
    low = (rest - middle.astype(f32)).astype(bf16)
    rows = x.shape[0]
    parts = jnp.dot(jnp.concatenate([high, middle, low], axis=0), picks.astype(bf16), preferred_element_type=f32)
    return parts[:rows] + (parts[rows : 2 * rows] + parts[2 * rows :])


def split3(matrix):
    high = matrix.astype(bf16)
    low = (matrix - high.astype(f32)).astype(bf16)
    return jnp.concatenate([high, low, high], axis=1)


def pack_x(rhs_hbm, areas_hbm, up_ref, down_ref, own_ref, rhs, areas, sems):
    copies = [
        pltpu.make_async_copy(rhs_hbm, rhs, sems.at[0]),
        pltpu.make_async_copy(areas_hbm, areas, sems.at[1]),
    ]
    for copy in copies:
        copy.start()
    for copy in copies:
        copy.wait()
    first = lax.broadcasted_iota(jnp.int32, (KA - K, 256), 0) == 0

    def area(x, beyond):
        return jnp.where(first, areas[x : x + 1, :], areas[beyond : beyond + 1, :])

    for x in range(8):
        for t in range(2):
            own_ref[x, :K, 128 * t : 128 * t + 128] = rhs[pl.ds(8 * t + x, K, stride=16), :]
        own_ref[x, K:, :] = area(x, x)
        if x < HX:
            down_ref[x, :K, :] = own_ref[x, :K, :]
            down_ref[x, K:, :] = area(x, x + HX)
        if x >= 8 - HX:
            up_ref[x - 8 + HX, :K, :] = own_ref[x, :K, :]
            up_ref[x - 8 + HX, K:, :] = area(x, x - HX)


def tables(stiff_ref, smooth_ref, vert_ref, retain_ref, weight_ref, lead, trail):
    scale = 7.5
    row = lax.broadcasted_iota(jnp.int32, (K, 128), 0)
    col = lax.broadcasted_iota(jnp.int32, (K, 128), 1)
    lane = lanes((1, 128))
    one = jnp.ones((1, 128), f32)
    zero = jnp.zeros((1, 128), f32)
    before, now, lead_row = zero, one, zero
    after, later, trail_row = zero, one, zero
    for k in range(K):
        lead[pl.ds(k, 1), :] = now
        lead_row = jnp.where(lane == k, now, lead_row)
        now, before = (stiff_ref[k] + 8.0) * (1.0 / scale) * now - (4.0 / scale**2) * before, now
        at = K - 1 - k
        trail[pl.ds(at, 1), :] = later
        trail_row = jnp.where(lane == at, later, trail_row)
        later, after = (stiff_ref[at] + 8.0) * (1.0 / scale) * later - (4.0 / scale**2) * after, later
    gap = jnp.abs(row - col)
    decay = jnp.ones((K, 128), f32)
    for b in range(6):
        decay = decay * jnp.where((gap >> b) & 1 == 1, (2.0 / scale) ** (1 << b), 1.0)
    upper = lead[...] * trail_row
    lower = lead_row * trail[...]
    inverse = decay * jnp.where(row <= col, upper, lower) / (scale * now)
    smooth_ref[...] = split3((0.4 * inverse)[:, :K])
    stiff_row = zero
    for k in range(K):
        stiff_row = jnp.where(lane == k, stiff_ref[k], stiff_row)
    diagonal = jnp.where(row == col, stiff_row, 0.0)
    stiff = jnp.broadcast_to(jnp.sum(diagonal, axis=1, keepdims=True), (K, 128))
    vert = jnp.where(row == col, stiff + 4.0, jnp.where(gap == 1, -2.0, 0.0))
    vert_ref[...] = split3(vert[:, :K])
    keep = jnp.sqrt(stiff + 0.25 * stiff * stiff) - 0.5 * stiff
    retain_ref[...] = 1.0 - keep
    weight_ref[...] = keep / (2.0 - keep)


def ext_row(own_ref, left_ref, right_ref, r):
    if r < HX:
        return left_ref[r]
    if r >= HX + 8:
        return right_ref[r - HX - 8]
    return own_ref[r - HX]


def whole_row(own_ref, left_ref, right_ref, tails_ref, r, levels=K):
    main = ext_row(own_ref, left_ref, right_ref, r)
    tail = tails_ref[r]
    at = slice(levels, levels + 1)
    return (
        jnp.concatenate([main[:K], tail[:K]], axis=1),
        jnp.concatenate([main[at], tail[at]], axis=1),
    )


def pack_y(own_ref, left_ref, right_ref, _, first_ref, second_ref):
    lane = lanes((KA, 128))
    low = high = jnp.zeros((KA, 128), f32)
    for r in range(NR):
        row = ext_row(own_ref, left_ref, right_ref, r)
        o = HY * r
        here = (lane >= o) & (lane < o + HY)
        low = jnp.where(here, pltpu.roll(row[:, :128], o, 1), low)
        high = jnp.where(here, pltpu.roll(row[:, 128:], o + HY, 1), high)
    even = lax.rem(lax.axis_index("narrow"), 2) == 0
    first_ref[...] = jnp.where(even, high, low)
    second_ref[...] = jnp.where(even, low, high)


def first_main(own_ref, left_ref, right_ref, smooth_ref, u1_ref):
    smooth = smooth_ref[...]
    for r in range(NR):
        u1_ref[r] = apply3(smooth, ext_row(own_ref, left_ref, right_ref, r)[:K])


def smooth_term(u, rhs, area, above, below, step):
    beside = above + below + pltpu.roll(u, step, 1) + pltpu.roll(u, LX - step, 1)
    return rhs - area * (4.0 * u - beside)


def pair_sum(v):
    even = lanes(v.shape) % 2 == 0
    return v + jnp.where(even, pltpu.roll(v, LX - 1, 1), pltpu.roll(v, 1, 1))


def pack_deep(u2_ref, coarse_ref, up_ref, down_ref):
    pack_side([u2_ref[x] for x in (5, 6, 7)], [coarse_ref[2], coarse_ref[3]], up_ref)
    pack_side([u2_ref[x] for x in (0, 1, 2)], [coarse_ref[0], coarse_ref[1]], down_ref)


def pack_side(rows, coarse, out_ref):
    lane = lanes((K, 128))
    even = lanes((K, LX)) % 2 == 0
    rows = rows + [jnp.where(even, coarse[0], coarse[1])]
    tails = jnp.zeros((K, 128), f32)
    for i, row in enumerate(rows):
        out_ref[2 * i] = row[:, :128]
        out_ref[2 * i + 1] = row[:, 128:256]
        here = (lane >= 16 * i) & (lane < 16 * i + 16)
        tails = jnp.where(here, pltpu.roll(row[:, 256:], HY + 16 * i, 1), tails)
    out_ref[8] = tails


def unpack_deep(got_ref):
    lane = lanes((K, 128))
    edge = (lane < HY) | (lane >= 128 - HY)
    rows = []
    for i in range(4):
        tail = jnp.where(edge, pltpu.roll(got_ref[8], 128 - HY - 16 * i, 1), 0.0)
        rows.append(jnp.concatenate([got_ref[2 * i], got_ref[2 * i + 1], tail], axis=1))
    both = rows.pop()
    even = lanes((K, LX)) % 2 == 0
    first = jnp.where(even, both, pltpu.roll(both, 1, 1))
    second = jnp.where(even, pltpu.roll(both, LX - 1, 1), both)
    return rows, (first, second)


def before_scan(
    own_ref, left_ref, right_ref, first_ref, second_ref, u1_ref, smooth_ref, vert_ref, retain_ref,
    sent_ref, tails_ref, u2_ref, coarse_ref, u1, fine,
):
    smooth = smooth_ref[...]
    lane = lanes((KA, 128))
    even = lax.rem(lax.axis_index("narrow"), 2) == 0
    low = jnp.where(even, first_ref[...], second_ref[...])
    high = jnp.where(even, second_ref[...], first_ref[...])
    tails = apply3(smooth, jnp.concatenate([low[:K], high[:K]], axis=1))

    def beyond(right, left, o):
        at = lane[: right.shape[0]]
        right = pltpu.roll(right, (128 - o) % 128, 1)
        left = pltpu.roll(left, 128 - HY - o, 1)
        return jnp.where(at < HY, right, jnp.where(at >= 128 - HY, left, 0.0))

    for r in range(NR):
        tails_ref[r] = beyond(low, high, HY * r)
        u1[r] = beyond(tails[:, :128], tails[:, 128:], HY * r)

    def row(r):
        return whole_row(own_ref, left_ref, right_ref, tails_ref, r)

    def first(r):
        return jnp.concatenate([u1_ref[r], u1[r]], axis=1)

    for r in range(1, NR - 1):
        u, (rhs, area) = first(r), row(r)
        term = smooth_term(u, rhs + 4.0 * u, area, first(r - 1), first(r + 1), 1)
        fine[r] = 0.6 * u + apply3(smooth, term)
    vert = vert_ref[...]
    for j in range(4):
        total, field = 0.0, 0.0
        for at in (2 * j + HX, 2 * j + HX + 1):
            u, (rhs, area) = fine[at], row(at)
            total += smooth_term(u, rhs, area, fine[at - 1], fine[at + 1], 1)
            field += u
        coarse_ref[j] = 0.25 * (pair_sum(total) - apply3(vert, pair_sum(field)))
    for x in range(8):
        u2_ref[x] = fine[x + HX]
    retain = wide3(retain_ref[...])
    ahead = coarse_ref[0]
    back = coarse_ref[3]
    for j in range(1, 4):
        ahead = retain * ahead + coarse_ref[j]
        back = retain * back + coarse_ref[3 - j]
    fine_lane = lax.broadcasted_iota(jnp.int32, (LX, 256), 0)
    coarse_lane = lax.broadcasted_iota(jnp.int32, (LX, 256), 1)
    pick = jnp.where(fine_lane == 2 * coarse_lane, 1.0, 0.0)
    both = select(jnp.concatenate([ahead, back], axis=0), pick)
    sent_ref[:, :128] = both[:K, :128]
    sent_ref[:, 128:256] = both[K:, :128]
    sent_ref[:, 256:] = both[:K, 128:] + pltpu.roll(both[K:, 128:], 64, 1)


def power(x, n):
    out = None
    while n:
        if n & 1:
            out = x if out is None else out * x
        x = x * x
        n >>= 1
    return out


def my_retain(retain_ref):
    at = lax.rem(lax.axis_index("wide"), PLANE)
    return retain_ref[pl.ds(pl.multiple_of(at * 8, 8), 8), :]


def plane_ends(blocks, retain):
    four = power(retain, 4)
    ends = []
    for order, part in ((range(PLANE), 0), (reversed(range(PLANE)), 1)):
        main, tail = 0.0, 0.0
        for m in order:
            main = four * main + blocks[m, :, 128 * part : 128 * part + 128]
            tail = four * tail + blocks[m, :, 256:]
        ends += [main, tail if part == 0 else pltpu.roll(tail, 64, 1)]
    return ends


def across_out(planes, blocks_ref, retain_ref, out_ref):
    retain = my_retain(retain_ref)
    here = lax.div(lax.axis_index("wide"), PLANE)
    ahead, ahead_tail, back, back_tail = plane_ends(blocks_ref, retain)
    reflect = power(retain, 33)
    step = power(retain, 64)
    for q in range(planes):
        reflect = jnp.where(q > here, reflect * step, reflect)
    back = back - reflect * ahead
    back_tail = back_tail - reflect * ahead_tail
    for q in range(planes):
        out_ref[q, :, :128] = jnp.where(q > here, ahead, back)
        out_ref[q, :, 128:] = jnp.where(q > here, ahead_tail, back_tail)


def across_in(planes, blocks_ref, others_ref, retain_ref, out_ref):
    retain = my_retain(retain_ref)
    here = lax.div(lax.axis_index("wide"), PLANE)
    ahead, ahead_tail, _, _ = plane_ends(blocks_ref, retain)
    four, plane = power(retain, 4), power(retain, 32)
    reflect, step = retain, power(retain, 64)
    enter, leave = [0.0, 0.0], [0.0, 0.0]
    for q in range(planes):
        reflect = jnp.where(q > here, reflect * step, reflect)
        back = planes - 1 - q
        for part in range(2):
            at = slice(128 * part, 128 * part + 128)
            enter[part] = jnp.where(q < here, plane * enter[part] + others_ref[q, :, at], enter[part])
            leave[part] = jnp.where(back > here, plane * leave[part] + others_ref[back, :, at], leave[part])
    leave[0] = leave[0] - reflect * (ahead + plane * enter[0])
    leave[1] = leave[1] - reflect * (ahead_tail + plane * enter[1])
    left = lanes((8, 128)) < 64
    leave[1] = pltpu.roll(leave[1], 64, 1)
    tails = []
    for m in range(PLANE):
        out_ref[m, :, :128] = enter[0]
        tails.append(enter[1])
        enter[0] = four * enter[0] + blocks_ref[m, :, :128]
        enter[1] = four * enter[1] + blocks_ref[m, :, 256:]
    for m in reversed(range(PLANE)):
        out_ref[m, :, 128:256] = leave[0]
        out_ref[m, :, 256:] = jnp.where(left, tails[m], leave[1])
        leave[0] = four * leave[0] + blocks_ref[m, :, 128:256]
        leave[1] = four * leave[1] + blocks_ref[m, :, 256:]


def after_scan(
    got_ref, own_ref, left_ref, right_ref, tails_ref, u2_ref, own_coarse_ref, deep_left, deep_right, smooth_ref, vert_ref, retain_ref, weight_ref,
    pressure_ref, residual_ref, coarse_ref, line, corr, ua, ub,
):
    left_rows, left_coarse = unpack_deep(deep_left)
    right_rows, right_coarse = unpack_deep(deep_right)
    for j in range(2):
        coarse_ref[j] = left_coarse[j]
        coarse_ref[6 + j] = right_coarse[j]
    for j in range(4):
        coarse_ref[2 + j] = own_coarse_ref[j]
    retain, weight = wide3(retain_ref[...]), wide3(weight_ref[...])
    inv_retain = 1.0 / retain
    coarse_lane = lax.broadcasted_iota(jnp.int32, (256, LX), 0)
    fine_lane = lax.broadcasted_iota(jnp.int32, (256, LX), 1)
    spread = jnp.where(fine_lane // 2 == coarse_lane, 1.0, 0.0)
    keep_left = lanes((K, 128)) < 64
    tail = got_ref[:, 256:]
    both = jnp.concatenate(
        [
            jnp.concatenate([got_ref[:, :128], jnp.where(keep_left, tail, 0.0)], axis=1),
            jnp.concatenate([got_ref[:, 128:256], jnp.where(keep_left, pltpu.roll(tail, 64, 1), 0.0)], axis=1),
        ],
        axis=0,
    )
    both = select(both, spread)

    def row(r, levels=K):
        return whole_row(own_ref, left_ref, right_ref, tails_ref, r, levels)

    def coef(j):
        if j == 0:
            pair = row(0, K + 1)[1] + row(1, K + 1)[1]
        elif j == 7:
            pair = row(NR - 2, K + 1)[1] + row(NR - 1, K + 1)[1]
        else:
            pair = row(2 * j + HX - 4)[1] + row(2 * j + HX - 3)[1]
        return 0.0625 * pair_sum(pair)

    coefs = [coef(j) for j in range(8)]
    enter, leave = both[:K], both[K:]
    reach = leave
    for j in (4, 5):
        reach = (reach - coarse_ref[j + 2]) * inv_retain
        line[j + 1 + 3] = reach
    reach = leave
    line[4 + 3] = reach
    for j in (3, 2, 1, 0, -1, -2):
        reach = coarse_ref[j + 2] + retain * reach
        line[j + 3] = reach
    ahead = (enter - coarse_ref[1]) * inv_retain
    ahead = (ahead - coarse_ref[0]) * inv_retain
    line[0] = jnp.where(coefs[0] > 0.0, weight * (ahead + retain * line[1]), 0.0)
    for j in range(-2, 7):
        inside = coefs[min(max(j + 2, 0), 7)] > 0.0
        start = retain * ahead
        line[j + 3] = jnp.where(inside, weight * (start + line[j + 3]), 0.0)
        if j < 6:
            ahead = enter if j == -1 else coarse_ref[j + 2] + start

    smooth = smooth_ref[...]

    for j in range(8):
        v = line[j + 1]
        term = smooth_term(v, coarse_ref[j] + 4.0 * v, coefs[j], line[j], line[j + 2], 2)
        corr[j] = 0.6 * v + apply3(smooth, term)
    for i in range(14):
        field = left_rows[i] if i < 3 else right_rows[i - 11] if i >= 11 else u2_ref[i - 3]
        ua[i] = field + corr[(i - 3) // 2 + 2]

    for source, target, least, most in ((ua, ub, 1, 13), (ub, ua, 2, 12)):
        for i in range(least, most):
            u, (rhs, area) = source[i], row(i + HX - 3)
            term = smooth_term(u, rhs + 4.0 * u, area, source[i - 1], source[i + 1], 1)
            target[i] = 0.6 * u + apply3(smooth, term)
    vert = vert_ref[...]
    for x in range(8):
        i = x + 3
        u = ua[i]
        rhs, area = row(x + HX)
        term = smooth_term(u, rhs, area, ua[i - 1], ua[i + 1], 1)
        rest = term[:, :256] - apply3(vert, u[:, :256])
        for t in range(2):
            here = pl.ds(8 * t + x, K, stride=16)
            pressure_ref[here, :] = u[:, 128 * t : 128 * t + 128]
            residual_ref[here, :] = rest[:, 128 * t : 128 * t + 128]


def local(rhs, areas, stiffness):
    wide, narrow = lax.axis_size("wide"), lax.axis_size("narrow")
    planes = wide // PLANE
    rhs = rhs.reshape(K, 8, 2, 128).transpose(0, 2, 1, 3).reshape(K * 16, 128)
    anywhere = [pl.BlockSpec(memory_space=pltpu.HBM)] * 2
    up, down, own = call(
        pack_x,
        [((HX, KA, 256), f32)] * 2 + [((8, KA, 256), f32)],
        [pltpu.VMEM((K * 16, 128), f32), pltpu.VMEM((8, 256), f32), pltpu.SemaphoreType.DMA((2,))],
        anywhere,
    )(rhs, areas)

    def shift(array, axis, count, by):
        pairs = [(i, i + by) for i in range(count) if 0 <= i + by < count]
        return lax.ppermute(array, axis, pairs)

    left = shift(up, "wide", wide, 1)
    right = shift(down, "wide", wide, -1)
    smooth, vert, retain, weight = call(
        tables,
        [((K, 192), bf16)] * 2 + [((K, 128), f32)] * 2,
        [pltpu.VMEM((K, 128), f32)] * 2,
        [pl.BlockSpec(memory_space=pltpu.SMEM)],
    )(stiffness)
    first, second = call(pack_y, [((KA, 128), f32)] * 2, specs=on_vmem(4))(own, left, right, retain)
    first = lax.ppermute(first, "narrow", [(i, i ^ 1) for i in range(narrow)])
    second = lax.ppermute(second, "narrow", [(i, ((i + 1) ^ 1) - 1) for i in range(1, narrow - 1)])
    (u1,) = call(first_main, [((NR, K, 256), f32)], specs=on_vmem(4))(own, left, right, smooth)
    sent, tails, u2, coarse = call(
        before_scan,
        K2_OUTS,
        K2_SCRATCH,
        on_vmem(9),
    )(own, left, right, first, second, u1, smooth, vert, retain)
    in_plane = [[p * PLANE + m for m in range(PLANE)] for p in range(planes)]
    over_planes = [[p * PLANE + m for p in range(planes)] for m in range(PLANE)]

    def exchange(array, groups):
        return lax.all_to_all(array, "wide", 0, 0, tiled=True, axis_index_groups=groups)

    blocks = exchange(sent.reshape(PLANE, 8, LX), in_plane)
    if DEEP_LATE:
        blocks, u2, coarse = lax.optimization_barrier((blocks, u2, coarse))
    deep_up, deep_down = call(pack_deep, [((9, K, 128), f32)] * 2, specs=on_vmem(2))(u2, coarse)
    deep_left = shift(deep_up, "wide", wide, 1)
    deep_right = shift(deep_down, "wide", wide, -1)
    (out,) = call(functools.partial(across_out, planes), [((planes, 8, 256), f32)], specs=on_vmem(2))(blocks, retain)
    others = exchange(out, over_planes)
    (back,) = call(functools.partial(across_in, planes), [((PLANE, 8, LX), f32)], specs=on_vmem(3))(
        blocks, others, retain
    )
    got = exchange(back, in_plane).reshape(K, LX)
    pressure, residual = call(
        after_scan,
        [((K * 16, 128), f32)] * 2,
        K4_SCRATCH,
        on_vmem(13),
    )(got, own, left, right, tails, u2, coarse, deep_left, deep_right, smooth, vert, retain, weight)
    return tuple(
        out.reshape(K, 2, 8, 128).transpose(0, 2, 1, 3).reshape(K, 8, 256) for out in (pressure, residual)
    )


def solution(mesh):
    placed = (P(None, "wide", "narrow"), P("wide", "narrow"), P())
    return jax.shard_map(
        local,
        mesh=mesh,
        in_specs=placed,
        out_specs=(P(None, "wide", "narrow"), P(None, "wide", "narrow")),
        check_vma=False,
    )
```

```python
import functools

import jax
import jax.numpy as jnp
from jax import lax
from jax.experimental import pallas as pl
from jax.experimental.pallas import tpu as pltpu
from jax.sharding import PartitionSpec as P

K = 64
KA = 72
HX = 2
HY = 8
NR = 8 + 2 * HX
LX = 384
PLANE = 8
f32, bf16 = jnp.float32, jnp.bfloat16
DEEP_LATE = True
K2_OUTS = [((K, LX), f32), ((NR, KA, 128), f32), ((8, K, LX), f32), ((4, K, LX), f32)]
K2_SCRATCH = [pltpu.VMEM((NR, K, 128), f32), pltpu.VMEM((NR, K, LX), f32)]
K4_SCRATCH = [pltpu.VMEM(s, f32) for s in ((8, K, LX), (10, K, LX), (8, K, LX), (14, K, LX), (14, K, LX))]
LIMIT = 16 * 1024 * 1024


def call(kernel, outs, scratch=(), specs=None):
    vmem = pl.BlockSpec(memory_space=pltpu.VMEM)
    return pl.pallas_call(
        kernel,
        out_shape=[jax.ShapeDtypeStruct(s, d) for s, d in outs],
        in_specs=specs,
        out_specs=[vmem] * len(outs),
        scratch_shapes=list(scratch),
        compiler_params=pltpu.CompilerParams(vmem_limit_bytes=LIMIT),
    )


def on_vmem(n):
    return [pl.BlockSpec(memory_space=pltpu.VMEM)] * n


def lanes(shape):
    return lax.broadcasted_iota(jnp.int32, shape, len(shape) - 1)


def wide3(table):
    return jnp.concatenate([table] * (LX // 128), axis=1)


def apply3(cat, x):
    high = x.astype(bf16)
    low = (x - high.astype(f32)).astype(bf16)
    return jnp.dot(cat, jnp.concatenate([high, high, low], axis=0), preferred_element_type=f32)


def select(x, picks):
    high = x.astype(bf16)
    rest = x - high.astype(f32)
    middle = rest.astype(bf16)
    low = (rest - middle.astype(f32)).astype(bf16)
    rows = x.shape[0]
    parts = jnp.dot(jnp.concatenate([high, middle, low], axis=0), picks.astype(bf16), preferred_element_type=f32)
    return parts[:rows] + (parts[rows : 2 * rows] + parts[2 * rows :])


def split3(matrix):
    high = matrix.astype(bf16)
    low = (matrix - high.astype(f32)).astype(bf16)
    return jnp.concatenate([high, low, high], axis=1)


def pack_x(rhs_hbm, areas_hbm, first_ref, second_ref, own_ref, rhs, areas, sems):
    copies = [
        pltpu.make_async_copy(rhs_hbm, rhs, sems.at[0]),
        pltpu.make_async_copy(areas_hbm, areas, sems.at[1]),
    ]
    for copy in copies:
        copy.start()
    for copy in copies:
        copy.wait()
    first = lax.broadcasted_iota(jnp.int32, (KA - K, 256), 0) == 0

    def area(x, beyond):
        return jnp.where(first, areas[x : x + 1, :], areas[beyond : beyond + 1, :])

    for x in range(8):
        for t in range(2):
            own_ref[x, :K, 128 * t : 128 * t + 128] = rhs[pl.ds(8 * t + x, K, stride=16), :]
        own_ref[x, K:, :] = area(x, x)
    even = lax.rem(lax.axis_index("wide"), 2) == 0
    for x in range(HX):
        up, down = own_ref[8 - HX + x, :K, :], own_ref[x, :K, :]
        up_area, down_area = area(8 - HX + x, 8 - 2 * HX + x), area(x, x + HX)
        first_ref[x, :K, :] = jnp.where(even, up, down)
        first_ref[x, K:, :] = jnp.where(even, up_area, down_area)
        second_ref[x, :K, :] = jnp.where(even, down, up)
        second_ref[x, K:, :] = jnp.where(even, down_area, up_area)


def tables(stiff_ref, smooth_ref, vert_ref, retain_ref, weight_ref, lead, trail):
    scale = 7.5
    row = lax.broadcasted_iota(jnp.int32, (K, 128), 0)
    col = lax.broadcasted_iota(jnp.int32, (K, 128), 1)
    lane = lanes((1, 128))
    one = jnp.ones((1, 128), f32)
    zero = jnp.zeros((1, 128), f32)
    before, now, lead_row = zero, one, zero
    after, later, trail_row = zero, one, zero
    for k in range(K):
        lead[pl.ds(k, 1), :] = now
        lead_row = jnp.where(lane == k, now, lead_row)
        now, before = (stiff_ref[k] + 8.0) * (1.0 / scale) * now - (4.0 / scale**2) * before, now
        at = K - 1 - k
        trail[pl.ds(at, 1), :] = later
        trail_row = jnp.where(lane == at, later, trail_row)
        later, after = (stiff_ref[at] + 8.0) * (1.0 / scale) * later - (4.0 / scale**2) * after, later
    gap = jnp.abs(row - col)
    decay = jnp.ones((K, 128), f32)
    for b in range(6):
        decay = decay * jnp.where((gap >> b) & 1 == 1, (2.0 / scale) ** (1 << b), 1.0)
    upper = lead[...] * trail_row
    lower = lead_row * trail[...]
    inverse = decay * jnp.where(row <= col, upper, lower) / (scale * now)
    smooth_ref[...] = split3((0.4 * inverse)[:, :K])
    stiff_row = zero
    for k in range(K):
        stiff_row = jnp.where(lane == k, stiff_ref[k], stiff_row)
    diagonal = jnp.where(row == col, stiff_row, 0.0)
    stiff = jnp.broadcast_to(jnp.sum(diagonal, axis=1, keepdims=True), (K, 128))
    vert = jnp.where(row == col, stiff + 4.0, jnp.where(gap == 1, -2.0, 0.0))
    vert_ref[...] = split3(vert[:, :K])
    keep = jnp.sqrt(stiff + 0.25 * stiff * stiff) - 0.5 * stiff
    retain_ref[...] = 1.0 - keep
    weight_ref[...] = keep / (2.0 - keep)


def ext_row(own_ref, left_ref, right_ref, r):
    if r < HX:
        return left_ref[r]
    if r >= HX + 8:
        return right_ref[r - HX - 8]
    return own_ref[r - HX]


def whole_row(own_ref, left_ref, right_ref, tails_ref, r, levels=K):
    main = ext_row(own_ref, left_ref, right_ref, r)
    tail = tails_ref[r]
    at = slice(levels, levels + 1)
    return (
        jnp.concatenate([main[:K], tail[:K]], axis=1),
        jnp.concatenate([main[at], tail[at]], axis=1),
    )


def pack_y(own_ref, x_second_ref, x_first_ref, _, first_ref, second_ref, left_ref, right_ref):
    even = lax.rem(lax.axis_index("wide"), 2) == 0
    left_ref[...] = jnp.where(even, x_second_ref[...], x_first_ref[...])
    right_ref[...] = jnp.where(even, x_first_ref[...], x_second_ref[...])
    lane = lanes((KA, 128))
    low = high = jnp.zeros((KA, 128), f32)
    for r in range(NR):
        row = ext_row(own_ref, left_ref, right_ref, r)
        o = HY * r
        here = (lane >= o) & (lane < o + HY)
        low = jnp.where(here, pltpu.roll(row[:, :128], o, 1), low)
        high = jnp.where(here, pltpu.roll(row[:, 128:], o + HY, 1), high)
    even = lax.rem(lax.axis_index("narrow"), 2) == 0
    first_ref[...] = jnp.where(even, high, low)
    second_ref[...] = jnp.where(even, low, high)


def first_main(own_ref, left_ref, right_ref, smooth_ref, u1_ref):
    smooth = smooth_ref[...]
    for r in range(NR):
        u1_ref[r] = apply3(smooth, ext_row(own_ref, left_ref, right_ref, r)[:K])


def smooth_term(u, rhs, area, above, below, step):
    beside = above + below + pltpu.roll(u, step, 1) + pltpu.roll(u, LX - step, 1)
    return rhs - area * (4.0 * u - beside)


def pair_sum(v):
    even = lanes(v.shape) % 2 == 0
    return v + jnp.where(even, pltpu.roll(v, LX - 1, 1), pltpu.roll(v, 1, 1))


def pack_deep(u2_ref, coarse_ref, up_ref, down_ref):
    pack_side([u2_ref[x] for x in (5, 6, 7)], [coarse_ref[2], coarse_ref[3]], up_ref)
    pack_side([u2_ref[x] for x in (0, 1, 2)], [coarse_ref[0], coarse_ref[1]], down_ref)


def pack_side(rows, coarse, out_ref):
    lane = lanes((K, 128))
    even = lanes((K, LX)) % 2 == 0
    rows = rows + [jnp.where(even, coarse[0], coarse[1])]
    tails = jnp.zeros((K, 128), f32)
    for i, row in enumerate(rows):
        out_ref[2 * i] = row[:, :128]
        out_ref[2 * i + 1] = row[:, 128:256]
        here = (lane >= 16 * i) & (lane < 16 * i + 16)
        tails = jnp.where(here, pltpu.roll(row[:, 256:], HY + 16 * i, 1), tails)
    out_ref[8] = tails


def unpack_deep(got_ref):
    lane = lanes((K, 128))
    edge = (lane < HY) | (lane >= 128 - HY)
    rows = []
    for i in range(4):
        tail = jnp.where(edge, pltpu.roll(got_ref[8], 128 - HY - 16 * i, 1), 0.0)
        rows.append(jnp.concatenate([got_ref[2 * i], got_ref[2 * i + 1], tail], axis=1))
    both = rows.pop()
    even = lanes((K, LX)) % 2 == 0
    first = jnp.where(even, both, pltpu.roll(both, 1, 1))
    second = jnp.where(even, pltpu.roll(both, LX - 1, 1), both)
    return rows, (first, second)


def before_scan(
    own_ref, left_ref, right_ref, second_ref, first_ref, u1_ref, smooth_ref, vert_ref, retain_ref,
    sent_ref, tails_ref, u2_ref, coarse_ref, u1, fine,
):
    smooth = smooth_ref[...]
    lane = lanes((KA, 128))
    even = lax.rem(lax.axis_index("narrow"), 2) == 0
    low = jnp.where(even, first_ref[...], second_ref[...])
    high = jnp.where(even, second_ref[...], first_ref[...])
    tails = apply3(smooth, jnp.concatenate([low[:K], high[:K]], axis=1))

    def beyond(right, left, o):
        at = lane[: right.shape[0]]
        right = pltpu.roll(right, (128 - o) % 128, 1)
        left = pltpu.roll(left, 128 - HY - o, 1)
        return jnp.where(at < HY, right, jnp.where(at >= 128 - HY, left, 0.0))

    for r in range(NR):
        tails_ref[r] = beyond(low, high, HY * r)
        u1[r] = beyond(tails[:, :128], tails[:, 128:], HY * r)

    def row(r):
        return whole_row(own_ref, left_ref, right_ref, tails_ref, r)

    def first(r):
        return jnp.concatenate([u1_ref[r], u1[r]], axis=1)

    for r in range(1, NR - 1):
        u, (rhs, area) = first(r), row(r)
        term = smooth_term(u, rhs + 4.0 * u, area, first(r - 1), first(r + 1), 1)
        fine[r] = 0.6 * u + apply3(smooth, term)
    vert = vert_ref[...]
    for j in range(4):
        total, field = 0.0, 0.0
        for at in (2 * j + HX, 2 * j + HX + 1):
            u, (rhs, area) = fine[at], row(at)
            total += smooth_term(u, rhs, area, fine[at - 1], fine[at + 1], 1)
            field += u
        coarse_ref[j] = 0.25 * (pair_sum(total) - apply3(vert, pair_sum(field)))
    for x in range(8):
        u2_ref[x] = fine[x + HX]
    retain = wide3(retain_ref[...])
    ahead = coarse_ref[0]
    back = coarse_ref[3]
    for j in range(1, 4):
        ahead = retain * ahead + coarse_ref[j]
        back = retain * back + coarse_ref[3 - j]
    fine_lane = lax.broadcasted_iota(jnp.int32, (LX, 256), 0)
    coarse_lane = lax.broadcasted_iota(jnp.int32, (LX, 256), 1)
    pick = jnp.where(fine_lane == 2 * coarse_lane, 1.0, 0.0)
    both = select(jnp.concatenate([ahead, back], axis=0), pick)
    sent_ref[:, :128] = both[:K, :128]
    sent_ref[:, 128:256] = both[K:, :128]
    sent_ref[:, 256:] = both[:K, 128:] + pltpu.roll(both[K:, 128:], 64, 1)


def power(x, n):
    out = None
    while n:
        if n & 1:
            out = x if out is None else out * x
        x = x * x
        n >>= 1
    return out


def my_retain(retain_ref):
    at = lax.rem(lax.axis_index("wide"), PLANE)
    return retain_ref[pl.ds(pl.multiple_of(at * 8, 8), 8), :]


def plane_ends(blocks, retain):
    four = power(retain, 4)
    ends = []
    for order, part in ((range(PLANE), 0), (reversed(range(PLANE)), 1)):
        main, tail = 0.0, 0.0
        for m in order:
            main = four * main + blocks[m, :, 128 * part : 128 * part + 128]
            tail = four * tail + blocks[m, :, 256:]
        ends += [main, tail if part == 0 else pltpu.roll(tail, 64, 1)]
    return ends


def across_out(planes, blocks_ref, retain_ref, out_ref):
    retain = my_retain(retain_ref)
    here = lax.div(lax.axis_index("wide"), PLANE)
    ahead, ahead_tail, back, back_tail = plane_ends(blocks_ref, retain)
    reflect = power(retain, 33)
    step = power(retain, 64)
    for q in range(planes):
        reflect = jnp.where(q > here, reflect * step, reflect)
    back = back - reflect * ahead
    back_tail = back_tail - reflect * ahead_tail
    for q in range(planes):
        out_ref[q, :, :128] = jnp.where(q > here, ahead, back)
        out_ref[q, :, 128:] = jnp.where(q > here, ahead_tail, back_tail)


def across_in(planes, blocks_ref, others_ref, retain_ref, out_ref):
    retain = my_retain(retain_ref)
    here = lax.div(lax.axis_index("wide"), PLANE)
    ahead, ahead_tail, _, _ = plane_ends(blocks_ref, retain)
    four, plane = power(retain, 4), power(retain, 32)
    reflect, step = retain, power(retain, 64)
    enter, leave = [0.0, 0.0], [0.0, 0.0]
    for q in range(planes):
        reflect = jnp.where(q > here, reflect * step, reflect)
        back = planes - 1 - q
        for part in range(2):
            at = slice(128 * part, 128 * part + 128)
            enter[part] = jnp.where(q < here, plane * enter[part] + others_ref[q, :, at], enter[part])
            leave[part] = jnp.where(back > here, plane * leave[part] + others_ref[back, :, at], leave[part])
    leave[0] = leave[0] - reflect * (ahead + plane * enter[0])
    leave[1] = leave[1] - reflect * (ahead_tail + plane * enter[1])
    left = lanes((8, 128)) < 64
    leave[1] = pltpu.roll(leave[1], 64, 1)
    tails = []
    for m in range(PLANE):
        out_ref[m, :, :128] = enter[0]
        tails.append(enter[1])
        enter[0] = four * enter[0] + blocks_ref[m, :, :128]
        enter[1] = four * enter[1] + blocks_ref[m, :, 256:]
    for m in reversed(range(PLANE)):
        out_ref[m, :, 128:256] = leave[0]
        out_ref[m, :, 256:] = jnp.where(left, tails[m], leave[1])
        leave[0] = four * leave[0] + blocks_ref[m, :, 128:256]
        leave[1] = four * leave[1] + blocks_ref[m, :, 256:]


def after_scan(
    got_ref, own_ref, left_ref, right_ref, tails_ref, u2_ref, own_coarse_ref, deep_left, deep_right, smooth_ref, vert_ref, retain_ref, weight_ref,
    pressure_ref, residual_ref, coarse_ref, line, corr, ua, ub,
):
    left_rows, left_coarse = unpack_deep(deep_left)
    right_rows, right_coarse = unpack_deep(deep_right)
    for j in range(2):
        coarse_ref[j] = left_coarse[j]
        coarse_ref[6 + j] = right_coarse[j]
    for j in range(4):
        coarse_ref[2 + j] = own_coarse_ref[j]
    retain, weight = wide3(retain_ref[...]), wide3(weight_ref[...])
    inv_retain = 1.0 / retain
    coarse_lane = lax.broadcasted_iota(jnp.int32, (256, LX), 0)
    fine_lane = lax.broadcasted_iota(jnp.int32, (256, LX), 1)
    spread = jnp.where(fine_lane // 2 == coarse_lane, 1.0, 0.0)
    keep_left = lanes((K, 128)) < 64
    tail = got_ref[:, 256:]
    both = jnp.concatenate(
        [
            jnp.concatenate([got_ref[:, :128], jnp.where(keep_left, tail, 0.0)], axis=1),
            jnp.concatenate([got_ref[:, 128:256], jnp.where(keep_left, pltpu.roll(tail, 64, 1), 0.0)], axis=1),
        ],
        axis=0,
    )
    both = select(both, spread)

    def row(r, levels=K):
        return whole_row(own_ref, left_ref, right_ref, tails_ref, r, levels)

    def coef(j):
        if j == 0:
            pair = row(0, K + 1)[1] + row(1, K + 1)[1]
        elif j == 7:
            pair = row(NR - 2, K + 1)[1] + row(NR - 1, K + 1)[1]
        else:
            pair = row(2 * j + HX - 4)[1] + row(2 * j + HX - 3)[1]
        return 0.0625 * pair_sum(pair)

    coefs = [coef(j) for j in range(8)]
    enter, leave = both[:K], both[K:]
    reach = leave
    for j in (4, 5):
        reach = (reach - coarse_ref[j + 2]) * inv_retain
        line[j + 1 + 3] = reach
    reach = leave
    line[4 + 3] = reach
    for j in (3, 2, 1, 0, -1, -2):
        reach = coarse_ref[j + 2] + retain * reach
        line[j + 3] = reach
    ahead = (enter - coarse_ref[1]) * inv_retain
    ahead = (ahead - coarse_ref[0]) * inv_retain
    line[0] = jnp.where(coefs[0] > 0.0, weight * (ahead + retain * line[1]), 0.0)
    for j in range(-2, 7):
        inside = coefs[min(max(j + 2, 0), 7)] > 0.0
        start = retain * ahead
        line[j + 3] = jnp.where(inside, weight * (start + line[j + 3]), 0.0)
        if j < 6:
            ahead = enter if j == -1 else coarse_ref[j + 2] + start

    smooth = smooth_ref[...]

    for j in range(8):
        v = line[j + 1]
        term = smooth_term(v, coarse_ref[j] + 4.0 * v, coefs[j], line[j], line[j + 2], 2)
        corr[j] = 0.6 * v + apply3(smooth, term)
    for i in range(14):
        field = left_rows[i] if i < 3 else right_rows[i - 11] if i >= 11 else u2_ref[i - 3]
        ua[i] = field + corr[(i - 3) // 2 + 2]

    for source, target, least, most in ((ua, ub, 1, 13), (ub, ua, 2, 12)):
        for i in range(least, most):
            u, (rhs, area) = source[i], row(i + HX - 3)
            term = smooth_term(u, rhs + 4.0 * u, area, source[i - 1], source[i + 1], 1)
            target[i] = 0.6 * u + apply3(smooth, term)
    vert = vert_ref[...]
    for x in range(8):
        i = x + 3
        u = ua[i]
        rhs, area = row(x + HX)
        term = smooth_term(u, rhs, area, ua[i - 1], ua[i + 1], 1)
        rest = term[:, :256] - apply3(vert, u[:, :256])
        for t in range(2):
            here = pl.ds(8 * t + x, K, stride=16)
            pressure_ref[here, :] = u[:, 128 * t : 128 * t + 128]
            residual_ref[here, :] = rest[:, 128 * t : 128 * t + 128]


def local(rhs, areas, stiffness):
    wide, narrow = lax.axis_size("wide"), lax.axis_size("narrow")
    planes = wide // PLANE
    rhs = rhs.reshape(K, 8, 2, 128).transpose(0, 2, 1, 3).reshape(K * 16, 128)
    anywhere = [pl.BlockSpec(memory_space=pltpu.HBM)] * 2
    up, down, own = call(
        pack_x,
        [((HX, KA, 256), f32)] * 2 + [((8, KA, 256), f32)],
        [pltpu.VMEM((K * 16, 128), f32), pltpu.VMEM((8, 256), f32), pltpu.SemaphoreType.DMA((2,))],
        anywhere,
    )(rhs, areas)

    def in_pairs(first, second, axis, count):
        second = lax.ppermute(second, axis, [(i, ((i + 1) ^ 1) - 1) for i in range(1, count - 1)])
        return lax.ppermute(first, axis, [(i, i ^ 1) for i in range(count)]), second

    def shift(array, axis, count, by):
        pairs = [(i, i + by) for i in range(count) if 0 <= i + by < count]
        return lax.ppermute(array, axis, pairs)

    x_first, x_second = in_pairs(up, down, "wide", wide)
    smooth, vert, retain, weight = call(
        tables,
        [((K, 192), bf16)] * 2 + [((K, 128), f32)] * 2,
        [pltpu.VMEM((K, 128), f32)] * 2,
        [pl.BlockSpec(memory_space=pltpu.SMEM)],
    )(stiffness)
    first, second, left, right = call(
        pack_y, [((KA, 128), f32)] * 2 + [((HX, KA, 256), f32)] * 2, specs=on_vmem(4)
    )(own, x_second, x_first, retain)
    first, second = in_pairs(first, second, "narrow", narrow)
    (u1,) = call(first_main, [((NR, K, 256), f32)], specs=on_vmem(4))(own, left, right, smooth)
    sent, tails, u2, coarse = call(
        before_scan,
        K2_OUTS,
        K2_SCRATCH,
        on_vmem(9),
    )(own, left, right, second, first, u1, smooth, vert, retain)
    in_plane = [[p * PLANE + m for m in range(PLANE)] for p in range(planes)]
    over_planes = [[p * PLANE + m for p in range(planes)] for m in range(PLANE)]

    def exchange(array, groups):
        return lax.all_to_all(array, "wide", 0, 0, tiled=True, axis_index_groups=groups)

    blocks = exchange(sent.reshape(PLANE, 8, LX), in_plane)
    if DEEP_LATE:
        blocks, u2, coarse = lax.optimization_barrier((blocks, u2, coarse))
    deep_up, deep_down = call(pack_deep, [((9, K, 128), f32)] * 2, specs=on_vmem(2))(u2, coarse)
    deep_left = shift(deep_up, "wide", wide, 1)
    deep_right = shift(deep_down, "wide", wide, -1)
    (out,) = call(functools.partial(across_out, planes), [((planes, 8, 256), f32)], specs=on_vmem(2))(blocks, retain)
    others = exchange(out, over_planes)
    (back,) = call(functools.partial(across_in, planes), [((PLANE, 8, LX), f32)], specs=on_vmem(3))(
        blocks, others, retain
    )
    got = exchange(back, in_plane).reshape(K, LX)
    pressure, residual = call(
        after_scan,
        [((K * 16, 128), f32)] * 2,
        K4_SCRATCH,
        on_vmem(13),
    )(got, own, left, right, tails, u2, coarse, deep_left, deep_right, smooth, vert, retain, weight)
    return tuple(
        out.reshape(K, 2, 8, 128).transpose(0, 2, 1, 3).reshape(K, 8, 256) for out in (pressure, residual)
    )


def solution(mesh):
    placed = (P(None, "wide", "narrow"), P("wide", "narrow"), P())
    return jax.shard_map(
        local,
        mesh=mesh,
        in_specs=placed,
        out_specs=(P(None, "wide", "narrow"), P(None, "wide", "narrow")),
        check_vma=False,
    )
```

```python
import functools

import jax
import jax.numpy as jnp
from jax import lax
from jax.experimental import pallas as pl
from jax.experimental.pallas import tpu as pltpu
from jax.sharding import PartitionSpec as P

K = 64
KA = 72
HX = 2
HY = 8
NR = 8 + 2 * HX
LX = 384
PLANE = 8
FIRST_M = 5
FIRST_Z = 8
f32, bf16 = jnp.float32, jnp.bfloat16
K2_OUTS = [((K, LX), f32), ((10, K, LX), f32), ((2, K, LX), f32)]
K2_SCRATCH = [pltpu.VMEM(s, f32) for s in ((NR, KA, 128), (NR, K, LX), (4, K, LX), (NR, K, 128))]
K4_SCRATCH = [
    pltpu.VMEM(s, f32)
    for s in ((NR, KA, 128), (8, K, LX), (10, K, LX), (8, K, LX), (14, K, LX), (14, K, LX))
]
LIMIT = 16 * 1024 * 1024


def call(kernel, outs, scratch=(), specs=None):
    vmem = pl.BlockSpec(memory_space=pltpu.VMEM)
    return pl.pallas_call(
        kernel,
        out_shape=[jax.ShapeDtypeStruct(s, d) for s, d in outs],
        in_specs=specs,
        out_specs=[vmem] * len(outs),
        scratch_shapes=list(scratch),
        compiler_params=pltpu.CompilerParams(vmem_limit_bytes=LIMIT),
    )


def on_vmem(n):
    return [pl.BlockSpec(memory_space=pltpu.VMEM)] * n


def lanes(shape):
    return lax.broadcasted_iota(jnp.int32, shape, len(shape) - 1)


def wide3(table):
    return jnp.concatenate([table] * (LX // 128), axis=1)


def apply3(cat, x):
    high = x.astype(bf16)
    low = (x - high.astype(f32)).astype(bf16)
    return jnp.dot(cat, jnp.concatenate([high, high, low], axis=0), preferred_element_type=f32)


def select(x, picks):
    high = x.astype(bf16)
    rest = x - high.astype(f32)
    middle = rest.astype(bf16)
    low = (rest - middle.astype(f32)).astype(bf16)
    rows = x.shape[0]
    parts = jnp.dot(jnp.concatenate([high, middle, low], axis=0), picks.astype(bf16), preferred_element_type=f32)
    return parts[:rows] + (parts[rows : 2 * rows] + parts[2 * rows :])


def split3(matrix):
    high = matrix.astype(bf16)
    low = (matrix - high.astype(f32)).astype(bf16)
    return jnp.concatenate([high, low, high], axis=1)


def pack_x(rhs_hbm, areas_hbm, first_ref, second_ref, own_ref, rhs, areas, sems):
    copies = [
        pltpu.make_async_copy(rhs_hbm, rhs, sems.at[0]),
        pltpu.make_async_copy(areas_hbm, areas, sems.at[1]),
    ]
    for copy in copies:
        copy.start()
    for copy in copies:
        copy.wait()
    first = lax.broadcasted_iota(jnp.int32, (KA - K, 256), 0) == 0

    def area(x, beyond):
        return jnp.where(first, areas[x : x + 1, :], areas[beyond : beyond + 1, :])

    for x in range(8):
        for t in range(2):
            own_ref[x, :K, 128 * t : 128 * t + 128] = rhs[pl.ds(8 * t + x, K, stride=16), :]
        own_ref[x, K:, :] = area(x, x)
    even = lax.rem(lax.axis_index("wide"), 2) == 0
    for x in range(HX):
        up, down = own_ref[8 - HX + x, :K, :], own_ref[x, :K, :]
        up_area, down_area = area(8 - HX + x, 8 - 2 * HX + x), area(x, x + HX)
        first_ref[x, :K, :] = jnp.where(even, up, down)
        first_ref[x, K:, :] = jnp.where(even, up_area, down_area)
        second_ref[x, :K, :] = jnp.where(even, down, up)
        second_ref[x, K:, :] = jnp.where(even, down_area, up_area)


def tables(stiff_ref, smooth_ref, vert_ref, retain_ref, weight_ref, lead, trail):
    scale = 7.5
    row = lax.broadcasted_iota(jnp.int32, (K, 128), 0)
    col = lax.broadcasted_iota(jnp.int32, (K, 128), 1)
    lane = lanes((1, 128))
    one = jnp.ones((1, 128), f32)
    zero = jnp.zeros((1, 128), f32)
    before, now, lead_row = zero, one, zero
    after, later, trail_row = zero, one, zero
    for k in range(K):
        lead[pl.ds(k, 1), :] = now
        lead_row = jnp.where(lane == k, now, lead_row)
        now, before = (stiff_ref[k] + 8.0) * (1.0 / scale) * now - (4.0 / scale**2) * before, now
        at = K - 1 - k
        trail[pl.ds(at, 1), :] = later
        trail_row = jnp.where(lane == at, later, trail_row)
        later, after = (stiff_ref[at] + 8.0) * (1.0 / scale) * later - (4.0 / scale**2) * after, later
    gap = jnp.abs(row - col)
    decay = jnp.ones((K, 128), f32)
    for b in range(6):
        decay = decay * jnp.where((gap >> b) & 1 == 1, (2.0 / scale) ** (1 << b), 1.0)
    upper = lead[...] * trail_row
    lower = lead_row * trail[...]
    inverse = decay * jnp.where(row <= col, upper, lower) / (scale * now)
    smooth_ref[...] = split3((0.4 * inverse)[:, :K])
    stiff_row = zero
    for k in range(K):
        stiff_row = jnp.where(lane == k, stiff_ref[k], stiff_row)
    diagonal = jnp.where(row == col, stiff_row, 0.0)
    stiff = jnp.broadcast_to(jnp.sum(diagonal, axis=1, keepdims=True), (K, 128))
    vert = jnp.where(row == col, stiff + 4.0, jnp.where(gap == 1, -2.0, 0.0))
    vert_ref[...] = split3(vert[:, :K])
    keep = jnp.sqrt(stiff + 0.25 * stiff * stiff) - 0.5 * stiff
    retain_ref[...] = 1.0 - keep
    weight_ref[...] = keep / (2.0 - keep)


def ext_row(own_ref, left_ref, right_ref, r):
    if r < HX:
        return left_ref[r]
    if r >= HX + 8:
        return right_ref[r - HX - 8]
    return own_ref[r - HX]


def whole_row(own_ref, left_ref, right_ref, tails_ref, r, levels=K):
    main = ext_row(own_ref, left_ref, right_ref, r)
    tail = tails_ref[r]
    at = slice(levels, levels + 1)
    return (
        jnp.concatenate([main[:K], tail[:K]], axis=1),
        jnp.concatenate([main[at], tail[at]], axis=1),
    )


def pack_y(own_ref, x_second_ref, x_first_ref, _, first_ref, second_ref, left_ref, right_ref):
    even = lax.rem(lax.axis_index("wide"), 2) == 0
    left_ref[...] = jnp.where(even, x_second_ref[...], x_first_ref[...])
    right_ref[...] = jnp.where(even, x_first_ref[...], x_second_ref[...])
    lane = lanes((KA, 128))
    low = high = jnp.zeros((KA, 128), f32)
    for r in range(NR):
        row = ext_row(own_ref, left_ref, right_ref, r)
        o = HY * r
        here = (lane >= o) & (lane < o + HY)
        low = jnp.where(here, pltpu.roll(row[:, :128], o, 1), low)
        high = jnp.where(here, pltpu.roll(row[:, 128:], o + HY, 1), high)
    even = lax.rem(lax.axis_index("narrow"), 2) == 0
    first_ref[...] = jnp.where(even, high, low)
    second_ref[...] = jnp.where(even, low, high)


def first_main(own_ref, left_ref, right_ref, smooth_ref, u1_ref):
    smooth = smooth_ref[...]
    for r in range(NR):
        u1_ref[r] = apply3(smooth, ext_row(own_ref, left_ref, right_ref, r)[:K])


def smooth_term(u, rhs, area, above, below, step):
    beside = above + below + pltpu.roll(u, step, 1) + pltpu.roll(u, LX - step, 1)
    return rhs - area * (4.0 * u - beside)


def pair_sum(v):
    even = lanes(v.shape) % 2 == 0
    return v + jnp.where(even, pltpu.roll(v, LX - 1, 1), pltpu.roll(v, 1, 1))


def y_sides(first_ref, second_ref):
    even = lax.rem(lax.axis_index("narrow"), 2) == 0
    first, second = first_ref[...], second_ref[...]
    return jnp.where(even, first, second), jnp.where(even, second, first)


def beyond(right, left, r):
    lane = lanes(right.shape)
    right = pltpu.roll(right, (128 - HY * r) % 128, 1)
    left = pltpu.roll(left, 128 - HY - HY * r, 1)
    return jnp.where(lane < HY, right, jnp.where(lane >= 128 - HY, left, 0.0))


def pack_deep(u2_ref, both_ref, first_ref, second_ref):
    lane = lanes((K, 128))
    even = lax.rem(lax.axis_index("wide"), 2) == 0
    tails = [jnp.zeros((K, 128), f32)] * 2
    for i in range(3):
        if i < 2:
            sides = u2_ref[6 + i], u2_ref[2 + i]
        else:
            sides = both_ref[1], both_ref[0]
        here = (lane >= 16 * i) & (lane < 16 * i + 16)
        rows = jnp.where(even, sides[0], sides[1]), jnp.where(even, sides[1], sides[0])
        for n, ref in enumerate((first_ref, second_ref)):
            ref[2 * i] = rows[n][:, :128]
            ref[2 * i + 1] = rows[n][:, 128:256]
            tails[n] = jnp.where(here, pltpu.roll(rows[n][:, 256:], HY + 16 * i, 1), tails[n])
    first_ref[6] = tails[0]
    second_ref[6] = tails[1]


def unpack_deep(got):
    lane = lanes((K, 128))
    edge = (lane < HY) | (lane >= 128 - HY)
    rows = []
    for i in range(3):
        tail = jnp.where(edge, pltpu.roll(got(6), 128 - HY - 16 * i, 1), 0.0)
        rows.append(jnp.concatenate([got(2 * i), got(2 * i + 1), tail], axis=1))
    return rows, unfold(rows.pop())


def unfold(both):
    even = lanes((K, LX)) % 2 == 0
    first = jnp.where(even, both, pltpu.roll(both, 1, 1))
    second = jnp.where(even, pltpu.roll(both, LX - 1, 1), both)
    return first, second


def before_scan(
    own_ref, left_ref, right_ref, second_ref, first_ref, u1_ref, smooth_ref, vert_ref, retain_ref,
    sent_ref, u2_ref, both_ref, tails_ref, fine, coarse_ref, u1,
):
    smooth = smooth_ref[...]
    low, high = y_sides(first_ref, second_ref)
    tails = apply3(smooth, jnp.concatenate([low[:K], high[:K]], axis=1))

    for r in range(NR):
        tails_ref[r] = beyond(low, high, r)
        u1[r] = beyond(tails[:, :128], tails[:, 128:], r)

    def row(r):
        return whole_row(own_ref, left_ref, right_ref, tails_ref, r)

    def first(r):
        return jnp.concatenate([u1_ref[r], u1[r]], axis=1)

    for r in range(1, NR - 1):
        u, (rhs, area) = first(r), row(r)
        term = smooth_term(u, rhs + 4.0 * u, area, first(r - 1), first(r + 1), 1)
        fine[r] = 0.6 * u + apply3(smooth, term)
    vert = vert_ref[...]
    for j in range(4):
        total, field = 0.0, 0.0
        for at in (2 * j + HX, 2 * j + HX + 1):
            u, (rhs, area) = fine[at], row(at)
            total += smooth_term(u, rhs, area, fine[at - 1], fine[at + 1], 1)
            field += u
        coarse_ref[j] = 0.25 * (pair_sum(total) - apply3(vert, pair_sum(field)))
    for x in range(10):
        u2_ref[x] = fine[x + 1]
    parity = lanes((K, LX)) % 2 == 0
    for j in range(2):
        both_ref[j] = jnp.where(parity, coarse_ref[2 * j], coarse_ref[2 * j + 1])
    retain = wide3(retain_ref[...])
    ahead = coarse_ref[0]
    back = coarse_ref[3]
    for j in range(1, 4):
        ahead = retain * ahead + coarse_ref[j]
        back = retain * back + coarse_ref[3 - j]
    fine_lane = lax.broadcasted_iota(jnp.int32, (LX, 256), 0)
    coarse_lane = lax.broadcasted_iota(jnp.int32, (LX, 256), 1)
    pick = jnp.where(fine_lane == 2 * coarse_lane, 1.0, 0.0)
    both = select(jnp.concatenate([ahead, back], axis=0), pick)
    sent_ref[:, :128] = both[:K, :128]
    sent_ref[:, 128:256] = both[K:, :128]
    sent_ref[:, 256:] = both[:K, 128:] + pltpu.roll(both[K:, 128:], 64, 1)


def power(x, n):
    out = None
    while n:
        if n & 1:
            out = x if out is None else out * x
        x = x * x
        n >>= 1
    return out


def my_retain(retain_ref):
    at = lax.rem(lax.axis_index("wide") + PLANE - FIRST_M, PLANE)
    return retain_ref[pl.ds(pl.multiple_of(at * 8, 8), 8), :]


def slot_m(m):
    return (m - FIRST_M) % PLANE


def slot_z(q, planes):
    return (q - FIRST_Z) % planes


def plane_ends(blocks, retain):
    four = power(retain, 4)
    ends = []
    for order, part in ((range(PLANE), 0), (reversed(range(PLANE)), 1)):
        main, tail = 0.0, 0.0
        for m in order:
            main = four * main + blocks[slot_m(m), :, 128 * part : 128 * part + 128]
            tail = four * tail + blocks[slot_m(m), :, 256:]
        ends += [main, tail if part == 0 else pltpu.roll(tail, 64, 1)]
    return ends


def across_out(planes, blocks_ref, retain_ref, out_ref):
    retain = my_retain(retain_ref)
    here = lax.div(lax.axis_index("wide"), PLANE)
    ahead, ahead_tail, back, back_tail = plane_ends(blocks_ref, retain)
    reflect = power(retain, 33)
    step = power(retain, 64)
    for q in range(planes):
        reflect = jnp.where(q > here, reflect * step, reflect)
    back = back - reflect * ahead
    back_tail = back_tail - reflect * ahead_tail
    for q in range(planes):
        out_ref[slot_z(q, planes), :, :128] = jnp.where(q > here, ahead, back)
        out_ref[slot_z(q, planes), :, 128:] = jnp.where(q > here, ahead_tail, back_tail)


def across_in(planes, blocks_ref, others_ref, retain_ref, out_ref):
    retain = my_retain(retain_ref)
    here = lax.div(lax.axis_index("wide"), PLANE)
    ahead, ahead_tail, _, _ = plane_ends(blocks_ref, retain)
    four, plane = power(retain, 4), power(retain, 32)
    reflect, step = retain, power(retain, 64)
    enter, leave = [0.0, 0.0], [0.0, 0.0]
    for q in range(planes):
        reflect = jnp.where(q > here, reflect * step, reflect)
        back = planes - 1 - q
        for part in range(2):
            at = slice(128 * part, 128 * part + 128)
            enter[part] = jnp.where(q < here, plane * enter[part] + others_ref[slot_z(q, planes), :, at], enter[part])
            leave[part] = jnp.where(back > here, plane * leave[part] + others_ref[slot_z(back, planes), :, at], leave[part])
    leave[0] = leave[0] - reflect * (ahead + plane * enter[0])
    leave[1] = leave[1] - reflect * (ahead_tail + plane * enter[1])
    left = lanes((8, 128)) < 64
    leave[1] = pltpu.roll(leave[1], 64, 1)
    tails = []
    for m in range(PLANE):
        out_ref[slot_m(m), :, :128] = enter[0]
        tails.append(enter[1])
        enter[0] = four * enter[0] + blocks_ref[slot_m(m), :, :128]
        enter[1] = four * enter[1] + blocks_ref[slot_m(m), :, 256:]
    for m in reversed(range(PLANE)):
        out_ref[slot_m(m), :, 128:256] = leave[0]
        out_ref[slot_m(m), :, 256:] = jnp.where(left, tails[m], leave[1])
        leave[0] = four * leave[0] + blocks_ref[slot_m(m), :, 128:256]
        leave[1] = four * leave[1] + blocks_ref[slot_m(m), :, 256:]


def after_scan(
    got_ref, own_ref, left_ref, right_ref, y_second_ref, y_first_ref, u2_ref, both_ref, deep_second_ref, deep_first_ref, smooth_ref, vert_ref, retain_ref, weight_ref,
    pressure_ref, residual_ref, tails_ref, coarse_ref, line, corr, ua, ub,
):
    even = lax.rem(lax.axis_index("wide"), 2) == 0
    left_rows, left_coarse = unpack_deep(lambda i: jnp.where(even, deep_second_ref[i], deep_first_ref[i]))
    right_rows, right_coarse = unpack_deep(lambda i: jnp.where(even, deep_first_ref[i], deep_second_ref[i]))
    for j in range(2):
        coarse_ref[j] = left_coarse[j]
        coarse_ref[6 + j] = right_coarse[j]
    for j in range(2):
        coarse_ref[2 + 2 * j], coarse_ref[3 + 2 * j] = unfold(both_ref[j])
    low, high = y_sides(y_first_ref, y_second_ref)
    for r in range(NR):
        tails_ref[r] = beyond(low, high, r)
    retain, weight = wide3(retain_ref[...]), wide3(weight_ref[...])
    inv_retain = 1.0 / retain
    coarse_lane = lax.broadcasted_iota(jnp.int32, (256, LX), 0)
    fine_lane = lax.broadcasted_iota(jnp.int32, (256, LX), 1)
    spread = jnp.where(fine_lane // 2 == coarse_lane, 1.0, 0.0)
    keep_left = lanes((K, 128)) < 64
    tail = got_ref[:, 256:]
    both = jnp.concatenate(
        [
            jnp.concatenate([got_ref[:, :128], jnp.where(keep_left, tail, 0.0)], axis=1),
            jnp.concatenate([got_ref[:, 128:256], jnp.where(keep_left, pltpu.roll(tail, 64, 1), 0.0)], axis=1),
        ],
        axis=0,
    )
    both = select(both, spread)

    def row(r, levels=K):
        return whole_row(own_ref, left_ref, right_ref, tails_ref, r, levels)

    def coef(j):
        if j == 0:
            pair = row(0, K + 1)[1] + row(1, K + 1)[1]
        elif j == 7:
            pair = row(NR - 2, K + 1)[1] + row(NR - 1, K + 1)[1]
        else:
            pair = row(2 * j + HX - 4)[1] + row(2 * j + HX - 3)[1]
        return 0.0625 * pair_sum(pair)

    coefs = [coef(j) for j in range(8)]
    enter, leave = both[:K], both[K:]
    reach = leave
    for j in (4, 5):
        reach = (reach - coarse_ref[j + 2]) * inv_retain
        line[j + 1 + 3] = reach
    reach = leave
    line[4 + 3] = reach
    for j in (3, 2, 1, 0, -1, -2):
        reach = coarse_ref[j + 2] + retain * reach
        line[j + 3] = reach
    ahead = (enter - coarse_ref[1]) * inv_retain
    ahead = (ahead - coarse_ref[0]) * inv_retain
    line[0] = jnp.where(coefs[0] > 0.0, weight * (ahead + retain * line[1]), 0.0)
    for j in range(-2, 7):
        inside = coefs[min(max(j + 2, 0), 7)] > 0.0
        start = retain * ahead
        line[j + 3] = jnp.where(inside, weight * (start + line[j + 3]), 0.0)
        if j < 6:
            ahead = enter if j == -1 else coarse_ref[j + 2] + start

    smooth = smooth_ref[...]

    for j in range(8):
        v = line[j + 1]
        term = smooth_term(v, coarse_ref[j] + 4.0 * v, coefs[j], line[j], line[j + 2], 2)
        corr[j] = 0.6 * v + apply3(smooth, term)
    for i in range(14):
        field = left_rows[i] if i < 2 else right_rows[i - 12] if i >= 12 else u2_ref[i - 2]
        ua[i] = field + corr[(i - 3) // 2 + 2]

    for source, target, least, most in ((ua, ub, 1, 13), (ub, ua, 2, 12)):
        for i in range(least, most):
            u, (rhs, area) = source[i], row(i + HX - 3)
            term = smooth_term(u, rhs + 4.0 * u, area, source[i - 1], source[i + 1], 1)
            target[i] = 0.6 * u + apply3(smooth, term)
    vert = vert_ref[...]
    for x in range(8):
        i = x + 3
        u = ua[i]
        rhs, area = row(x + HX)
        term = smooth_term(u, rhs, area, ua[i - 1], ua[i + 1], 1)
        rest = term[:, :256] - apply3(vert, u[:, :256])
        for t in range(2):
            here = pl.ds(8 * t + x, K, stride=16)
            pressure_ref[here, :] = u[:, 128 * t : 128 * t + 128]
            residual_ref[here, :] = rest[:, 128 * t : 128 * t + 128]


def local(rhs, areas, stiffness):
    wide, narrow = lax.axis_size("wide"), lax.axis_size("narrow")
    planes = wide // PLANE
    rhs = rhs.reshape(K, 8, 2, 128).transpose(0, 2, 1, 3).reshape(K * 16, 128)
    anywhere = [pl.BlockSpec(memory_space=pltpu.HBM)] * 2
    up, down, own = call(
        pack_x,
        [((HX, KA, 256), f32)] * 2 + [((8, KA, 256), f32)],
        [pltpu.VMEM((K * 16, 128), f32), pltpu.VMEM((8, 256), f32), pltpu.SemaphoreType.DMA((2,))],
        anywhere,
    )(rhs, areas)

    def in_pairs(first, second, axis, count):
        second = lax.ppermute(second, axis, [(i, ((i + 1) ^ 1) - 1) for i in range(1, count - 1)])
        return lax.ppermute(first, axis, [(i, i ^ 1) for i in range(count)]), second

    x_first, x_second = in_pairs(up, down, "wide", wide)
    smooth, vert, retain, weight = call(
        tables,
        [((K, 192), bf16)] * 2 + [((K, 128), f32)] * 2,
        [pltpu.VMEM((K, 128), f32)] * 2,
        [pl.BlockSpec(memory_space=pltpu.SMEM)],
    )(stiffness)
    first, second, left, right = call(
        pack_y, [((KA, 128), f32)] * 2 + [((HX, KA, 256), f32)] * 2, specs=on_vmem(4)
    )(own, x_second, x_first, retain)
    first, second = in_pairs(first, second, "narrow", narrow)
    (u1,) = call(first_main, [((NR, K, 256), f32)], specs=on_vmem(4))(own, left, right, smooth)
    sent, u2, coarse = call(
        before_scan,
        K2_OUTS,
        K2_SCRATCH,
        on_vmem(9),
    )(own, left, right, second, first, u1, smooth, vert, retain)
    in_plane = [[p * PLANE + (s + FIRST_M) % PLANE for s in range(PLANE)] for p in range(planes)]
    over_planes = [[(s + FIRST_Z) % planes * PLANE + m for s in range(planes)] for m in range(PLANE)]

    def exchange(array, groups):
        return lax.all_to_all(array, "wide", 0, 0, tiled=True, axis_index_groups=groups)

    blocks = exchange(sent.reshape(PLANE, 8, LX), in_plane)
    blocks, u2, coarse = lax.optimization_barrier((blocks, u2, coarse))
    deep_first, deep_second = call(pack_deep, [((7, K, 128), f32)] * 2, specs=on_vmem(2))(u2, coarse)
    deep_first, deep_second = in_pairs(deep_first, deep_second, "wide", wide)
    (out,) = call(functools.partial(across_out, planes), [((planes, 8, 256), f32)], specs=on_vmem(2))(blocks, retain)
    others = exchange(out, over_planes)
    (back,) = call(functools.partial(across_in, planes), [((PLANE, 8, LX), f32)], specs=on_vmem(3))(
        blocks, others, retain
    )
    got = exchange(back, in_plane).reshape(K, LX)
    pressure, residual = call(
        after_scan,
        [((K * 16, 128), f32)] * 2,
        K4_SCRATCH,
        on_vmem(14),
    )(got, own, left, right, second, first, u2, coarse, deep_second, deep_first, smooth, vert, retain, weight)
    return tuple(
        out.reshape(K, 2, 8, 128).transpose(0, 2, 1, 3).reshape(K, 8, 256) for out in (pressure, residual)
    )


def solution(mesh):
    placed = (P(None, "wide", "narrow"), P("wide", "narrow"), P())
    return jax.shard_map(
        local,
        mesh=mesh,
        in_specs=placed,
        out_specs=(P(None, "wide", "narrow"), P(None, "wide", "narrow")),
        check_vma=False,
    )
```

```python
import functools

import jax
import jax.numpy as jnp
from jax import lax
from jax.experimental import pallas as pl
from jax.experimental.pallas import tpu as pltpu
from jax.sharding import PartitionSpec as P

K = 64
KA = 72
HX = 2
HY = 8
NR = 8 + 2 * HX
LX = 384
PLANE = 8
FIRST_M = 4
FIRST_Z = 10
f32, bf16 = jnp.float32, jnp.bfloat16
K2_OUTS = [((K, LX), f32), ((10, K, LX), f32), ((2, K, LX), f32)]
K2_SCRATCH = [pltpu.VMEM(s, f32) for s in ((NR, KA, 128), (NR, K, LX), (4, K, LX), (NR, K, 128))]
K4_SCRATCH = [
    pltpu.VMEM(s, f32)
    for s in ((NR, KA, 128), (8, K, LX), (10, K, LX), (8, K, LX), (14, K, LX), (14, K, LX))
]
LIMIT = 16 * 1024 * 1024


def call(kernel, outs, scratch=(), specs=None):
    vmem = pl.BlockSpec(memory_space=pltpu.VMEM)
    return pl.pallas_call(
        kernel,
        out_shape=[jax.ShapeDtypeStruct(s, d) for s, d in outs],
        in_specs=specs,
        out_specs=[vmem] * len(outs),
        scratch_shapes=list(scratch),
        compiler_params=pltpu.CompilerParams(vmem_limit_bytes=LIMIT),
    )


def on_vmem(n):
    return [pl.BlockSpec(memory_space=pltpu.VMEM)] * n


def lanes(shape):
    return lax.broadcasted_iota(jnp.int32, shape, len(shape) - 1)


def wide3(table):
    return jnp.concatenate([table] * (LX // 128), axis=1)


def apply3(cat, x):
    high = x.astype(bf16)
    low = (x - high.astype(f32)).astype(bf16)
    return jnp.dot(cat, jnp.concatenate([high, high, low], axis=0), preferred_element_type=f32)


def select(x, picks):
    high = x.astype(bf16)
    rest = x - high.astype(f32)
    middle = rest.astype(bf16)
    low = (rest - middle.astype(f32)).astype(bf16)
    rows = x.shape[0]
    parts = jnp.dot(jnp.concatenate([high, middle, low], axis=0), picks.astype(bf16), preferred_element_type=f32)
    return parts[:rows] + (parts[rows : 2 * rows] + parts[2 * rows :])


def split3(matrix):
    high = matrix.astype(bf16)
    low = (matrix - high.astype(f32)).astype(bf16)
    return jnp.concatenate([high, low, high], axis=1)


def pack_x(rhs_hbm, areas_hbm, first_ref, second_ref, own_ref, rhs, areas, sems):
    copies = [
        pltpu.make_async_copy(rhs_hbm, rhs, sems.at[0]),
        pltpu.make_async_copy(areas_hbm, areas, sems.at[1]),
    ]
    for copy in copies:
        copy.start()
    for copy in copies:
        copy.wait()
    first = lax.broadcasted_iota(jnp.int32, (KA - K, 256), 0) == 0

    def area(x, beyond):
        return jnp.where(first, areas[x : x + 1, :], areas[beyond : beyond + 1, :])

    for x in range(8):
        for t in range(2):
            own_ref[x, :K, 128 * t : 128 * t + 128] = rhs[pl.ds(8 * t + x, K, stride=16), :]
        own_ref[x, K:, :] = area(x, x)
    even = lax.rem(lax.axis_index("wide"), 2) == 0
    for x in range(HX):
        up, down = own_ref[8 - HX + x, :K, :], own_ref[x, :K, :]
        up_area, down_area = area(8 - HX + x, 8 - 2 * HX + x), area(x, x + HX)
        first_ref[x, :K, :] = jnp.where(even, up, down)
        first_ref[x, K:, :] = jnp.where(even, up_area, down_area)
        second_ref[x, :K, :] = jnp.where(even, down, up)
        second_ref[x, K:, :] = jnp.where(even, down_area, up_area)


def tables(stiff_ref, smooth_ref, vert_ref, retain_ref, weight_ref, lead, trail):
    scale = 7.5
    row = lax.broadcasted_iota(jnp.int32, (K, 128), 0)
    col = lax.broadcasted_iota(jnp.int32, (K, 128), 1)
    lane = lanes((1, 128))
    one = jnp.ones((1, 128), f32)
    zero = jnp.zeros((1, 128), f32)
    before, now, lead_row = zero, one, zero
    after, later, trail_row = zero, one, zero
    for k in range(K):
        lead[pl.ds(k, 1), :] = now
        lead_row = jnp.where(lane == k, now, lead_row)
        now, before = (stiff_ref[k] + 8.0) * (1.0 / scale) * now - (4.0 / scale**2) * before, now
        at = K - 1 - k
        trail[pl.ds(at, 1), :] = later
        trail_row = jnp.where(lane == at, later, trail_row)
        later, after = (stiff_ref[at] + 8.0) * (1.0 / scale) * later - (4.0 / scale**2) * after, later
    gap = jnp.abs(row - col)
    decay = jnp.ones((K, 128), f32)
    for b in range(6):
        decay = decay * jnp.where((gap >> b) & 1 == 1, (2.0 / scale) ** (1 << b), 1.0)
    upper = lead[...] * trail_row
    lower = lead_row * trail[...]
    inverse = decay * jnp.where(row <= col, upper, lower) / (scale * now)
    smooth_ref[...] = split3((0.4 * inverse)[:, :K])
    stiff_row = zero
    for k in range(K):
        stiff_row = jnp.where(lane == k, stiff_ref[k], stiff_row)
    diagonal = jnp.where(row == col, stiff_row, 0.0)
    stiff = jnp.broadcast_to(jnp.sum(diagonal, axis=1, keepdims=True), (K, 128))
    vert = jnp.where(row == col, stiff + 4.0, jnp.where(gap == 1, -2.0, 0.0))
    vert_ref[...] = split3(vert[:, :K])
    keep = jnp.sqrt(stiff + 0.25 * stiff * stiff) - 0.5 * stiff
    retain_ref[...] = 1.0 - keep
    weight_ref[...] = keep / (2.0 - keep)


def ext_row(own_ref, left_ref, right_ref, r):
    if r < HX:
        return left_ref[r]
    if r >= HX + 8:
        return right_ref[r - HX - 8]
    return own_ref[r - HX]


def whole_row(own_ref, left_ref, right_ref, tails_ref, r, levels=K):
    main = ext_row(own_ref, left_ref, right_ref, r)
    tail = tails_ref[r]
    at = slice(levels, levels + 1)
    return (
        jnp.concatenate([main[:K], tail[:K]], axis=1),
        jnp.concatenate([main[at], tail[at]], axis=1),
    )


def pack_y(own_ref, x_second_ref, x_first_ref, _, first_ref, second_ref, left_ref, right_ref):
    even = lax.rem(lax.axis_index("wide"), 2) == 0
    left_ref[...] = jnp.where(even, x_second_ref[...], x_first_ref[...])
    right_ref[...] = jnp.where(even, x_first_ref[...], x_second_ref[...])
    lane = lanes((KA, 128))
    low = high = jnp.zeros((KA, 128), f32)
    for r in range(NR):
        row = ext_row(own_ref, left_ref, right_ref, r)
        o = HY * r
        here = (lane >= o) & (lane < o + HY)
        low = jnp.where(here, pltpu.roll(row[:, :128], o, 1), low)
        high = jnp.where(here, pltpu.roll(row[:, 128:], o + HY, 1), high)
    even = lax.rem(lax.axis_index("narrow"), 2) == 0
    first_ref[...] = jnp.where(even, high, low)
    second_ref[...] = jnp.where(even, low, high)


def first_main(own_ref, left_ref, right_ref, smooth_ref, u1_ref):
    smooth = smooth_ref[...]
    for r in range(NR):
        u1_ref[r] = apply3(smooth, ext_row(own_ref, left_ref, right_ref, r)[:K])


def smooth_term(u, rhs, area, above, below, step):
    beside = above + below + pltpu.roll(u, step, 1) + pltpu.roll(u, LX - step, 1)
    return rhs - area * (4.0 * u - beside)


def pair_sum(v):
    even = lanes(v.shape) % 2 == 0
    return v + jnp.where(even, pltpu.roll(v, LX - 1, 1), pltpu.roll(v, 1, 1))


def y_sides(first_ref, second_ref):
    even = lax.rem(lax.axis_index("narrow"), 2) == 0
    first, second = first_ref[...], second_ref[...]
    return jnp.where(even, first, second), jnp.where(even, second, first)


def beyond(right, left, r):
    lane = lanes(right.shape)
    right = pltpu.roll(right, (128 - HY * r) % 128, 1)
    left = pltpu.roll(left, 128 - HY - HY * r, 1)
    return jnp.where(lane < HY, right, jnp.where(lane >= 128 - HY, left, 0.0))


def pack_deep(u2_ref, both_ref, first_ref, second_ref):
    lane = lanes((K, 128))
    even = lax.rem(lax.axis_index("wide"), 2) == 0
    tails = [jnp.zeros((K, 128), f32)] * 2
    for i in range(3):
        if i < 2:
            sides = u2_ref[6 + i], u2_ref[2 + i]
        else:
            sides = both_ref[1], both_ref[0]
        here = (lane >= 16 * i) & (lane < 16 * i + 16)
        rows = jnp.where(even, sides[0], sides[1]), jnp.where(even, sides[1], sides[0])
        for n, ref in enumerate((first_ref, second_ref)):
            ref[2 * i] = rows[n][:, :128]
            ref[2 * i + 1] = rows[n][:, 128:256]
            tails[n] = jnp.where(here, pltpu.roll(rows[n][:, 256:], HY + 16 * i, 1), tails[n])
    first_ref[6] = tails[0]
    second_ref[6] = tails[1]


def unpack_deep(got):
    lane = lanes((K, 128))
    edge = (lane < HY) | (lane >= 128 - HY)
    rows = []
    for i in range(3):
        tail = jnp.where(edge, pltpu.roll(got(6), 128 - HY - 16 * i, 1), 0.0)
        rows.append(jnp.concatenate([got(2 * i), got(2 * i + 1), tail], axis=1))
    return rows, unfold(rows.pop())


def unfold(both):
    even = lanes((K, LX)) % 2 == 0
    first = jnp.where(even, both, pltpu.roll(both, 1, 1))
    second = jnp.where(even, pltpu.roll(both, LX - 1, 1), both)
    return first, second


def before_scan(
    own_ref, left_ref, right_ref, second_ref, first_ref, u1_ref, smooth_ref, vert_ref, retain_ref,
    sent_ref, u2_ref, both_ref, tails_ref, fine, coarse_ref, u1,
):
    smooth = smooth_ref[...]
    low, high = y_sides(first_ref, second_ref)
    tails = apply3(smooth, jnp.concatenate([low[:K], high[:K]], axis=1))

    for r in range(NR):
        tails_ref[r] = beyond(low, high, r)
        u1[r] = beyond(tails[:, :128], tails[:, 128:], r)

    def row(r):
        return whole_row(own_ref, left_ref, right_ref, tails_ref, r)

    def first(r):
        return jnp.concatenate([u1_ref[r], u1[r]], axis=1)

    for r in range(1, NR - 1):
        u, (rhs, area) = first(r), row(r)
        term = smooth_term(u, rhs + 4.0 * u, area, first(r - 1), first(r + 1), 1)
        fine[r] = 0.6 * u + apply3(smooth, term)
    vert = vert_ref[...]
    for j in range(4):
        total, field = 0.0, 0.0
        for at in (2 * j + HX, 2 * j + HX + 1):
            u, (rhs, area) = fine[at], row(at)
            total += smooth_term(u, rhs, area, fine[at - 1], fine[at + 1], 1)
            field += u
        coarse_ref[j] = 0.25 * (pair_sum(total) - apply3(vert, pair_sum(field)))
    for x in range(10):
        u2_ref[x] = fine[x + 1]
    parity = lanes((K, LX)) % 2 == 0
    for j in range(2):
        both_ref[j] = jnp.where(parity, coarse_ref[2 * j], coarse_ref[2 * j + 1])
    retain = wide3(retain_ref[...])
    ahead = coarse_ref[0]
    back = coarse_ref[3]
    for j in range(1, 4):
        ahead = retain * ahead + coarse_ref[j]
        back = retain * back + coarse_ref[3 - j]
    fine_lane = lax.broadcasted_iota(jnp.int32, (LX, 256), 0)
    coarse_lane = lax.broadcasted_iota(jnp.int32, (LX, 256), 1)
    pick = jnp.where(fine_lane == 2 * coarse_lane, 1.0, 0.0)
    both = select(jnp.concatenate([ahead, back], axis=0), pick)
    sent_ref[:, :128] = both[:K, :128]
    sent_ref[:, 128:256] = both[K:, :128]
    sent_ref[:, 256:] = both[:K, 128:] + pltpu.roll(both[K:, 128:], 64, 1)


def power(x, n):
    out = None
    while n:
        if n & 1:
            out = x if out is None else out * x
        x = x * x
        n >>= 1
    return out


def my_retain(retain_ref):
    at = lax.rem(lax.axis_index("wide") + PLANE - FIRST_M, PLANE)
    return retain_ref[pl.ds(pl.multiple_of(at * 8, 8), 8), :]


def slot_m(m):
    return (m - FIRST_M) % PLANE


def slot_z(q, planes):
    return (q - FIRST_Z) % planes


def plane_ends(blocks, retain):
    four = power(retain, 4)
    ends = []
    for order, part in ((range(PLANE), 0), (reversed(range(PLANE)), 1)):
        main, tail = 0.0, 0.0
        for m in order:
            main = four * main + blocks[slot_m(m), :, 128 * part : 128 * part + 128]
            tail = four * tail + blocks[slot_m(m), :, 256:]
        ends += [main, tail if part == 0 else pltpu.roll(tail, 64, 1)]
    return ends


def across_out(planes, blocks_ref, retain_ref, out_ref):
    retain = my_retain(retain_ref)
    here = lax.div(lax.axis_index("wide"), PLANE)
    ahead, ahead_tail, back, back_tail = plane_ends(blocks_ref, retain)
    reflect = power(retain, 33)
    step = power(retain, 64)
    for q in range(planes):
        reflect = jnp.where(q > here, reflect * step, reflect)
    back = back - reflect * ahead
    back_tail = back_tail - reflect * ahead_tail
    for q in range(planes):
        out_ref[slot_z(q, planes), :, :128] = jnp.where(q > here, ahead, back)
        out_ref[slot_z(q, planes), :, 128:] = jnp.where(q > here, ahead_tail, back_tail)


def across_in(planes, blocks_ref, others_ref, retain_ref, out_ref):
    retain = my_retain(retain_ref)
    here = lax.div(lax.axis_index("wide"), PLANE)
    ahead, ahead_tail, _, _ = plane_ends(blocks_ref, retain)
    four, plane = power(retain, 4), power(retain, 32)
    reflect, step = retain, power(retain, 64)
    enter, leave = [0.0, 0.0], [0.0, 0.0]
    for q in range(planes):
        reflect = jnp.where(q > here, reflect * step, reflect)
        back = planes - 1 - q
        for part in range(2):
            at = slice(128 * part, 128 * part + 128)
            enter[part] = jnp.where(q < here, plane * enter[part] + others_ref[slot_z(q, planes), :, at], enter[part])
            leave[part] = jnp.where(back > here, plane * leave[part] + others_ref[slot_z(back, planes), :, at], leave[part])
    leave[0] = leave[0] - reflect * (ahead + plane * enter[0])
    leave[1] = leave[1] - reflect * (ahead_tail + plane * enter[1])
    left = lanes((8, 128)) < 64
    leave[1] = pltpu.roll(leave[1], 64, 1)
    tails = []
    for m in range(PLANE):
        out_ref[slot_m(m), :, :128] = enter[0]
        tails.append(enter[1])
        enter[0] = four * enter[0] + blocks_ref[slot_m(m), :, :128]
        enter[1] = four * enter[1] + blocks_ref[slot_m(m), :, 256:]
    for m in reversed(range(PLANE)):
        out_ref[slot_m(m), :, 128:256] = leave[0]
        out_ref[slot_m(m), :, 256:] = jnp.where(left, tails[m], leave[1])
        leave[0] = four * leave[0] + blocks_ref[slot_m(m), :, 128:256]
        leave[1] = four * leave[1] + blocks_ref[slot_m(m), :, 256:]


def after_scan(
    got_ref, own_ref, left_ref, right_ref, y_second_ref, y_first_ref, u2_ref, both_ref, deep_first_ref, deep_second_ref, smooth_ref, vert_ref, retain_ref, weight_ref,
    pressure_ref, residual_ref, tails_ref, coarse_ref, line, corr, ua, ub,
):
    even = lax.rem(lax.axis_index("wide"), 2) == 0
    left_rows, left_coarse = unpack_deep(lambda i: jnp.where(even, deep_second_ref[i], deep_first_ref[i]))
    right_rows, right_coarse = unpack_deep(lambda i: jnp.where(even, deep_first_ref[i], deep_second_ref[i]))
    for j in range(2):
        coarse_ref[j] = left_coarse[j]
        coarse_ref[6 + j] = right_coarse[j]
    for j in range(2):
        coarse_ref[2 + 2 * j], coarse_ref[3 + 2 * j] = unfold(both_ref[j])
    low, high = y_sides(y_first_ref, y_second_ref)
    for r in range(NR):
        tails_ref[r] = beyond(low, high, r)
    retain, weight = wide3(retain_ref[...]), wide3(weight_ref[...])
    inv_retain = 1.0 / retain
    coarse_lane = lax.broadcasted_iota(jnp.int32, (256, LX), 0)
    fine_lane = lax.broadcasted_iota(jnp.int32, (256, LX), 1)
    spread = jnp.where(fine_lane // 2 == coarse_lane, 1.0, 0.0)
    keep_left = lanes((K, 128)) < 64
    tail = got_ref[:, 256:]
    both = jnp.concatenate(
        [
            jnp.concatenate([got_ref[:, :128], jnp.where(keep_left, tail, 0.0)], axis=1),
            jnp.concatenate([got_ref[:, 128:256], jnp.where(keep_left, pltpu.roll(tail, 64, 1), 0.0)], axis=1),
        ],
        axis=0,
    )
    both = select(both, spread)

    def row(r, levels=K):
        return whole_row(own_ref, left_ref, right_ref, tails_ref, r, levels)

    def coef(j):
        if j == 0:
            pair = row(0, K + 1)[1] + row(1, K + 1)[1]
        elif j == 7:
            pair = row(NR - 2, K + 1)[1] + row(NR - 1, K + 1)[1]
        else:
            pair = row(2 * j + HX - 4)[1] + row(2 * j + HX - 3)[1]
        return 0.0625 * pair_sum(pair)

    coefs = [coef(j) for j in range(8)]
    enter, leave = both[:K], both[K:]
    reach = leave
    for j in (4, 5):
        reach = (reach - coarse_ref[j + 2]) * inv_retain
        line[j + 1 + 3] = reach
    reach = leave
    line[4 + 3] = reach
    for j in (3, 2, 1, 0, -1, -2):
        reach = coarse_ref[j + 2] + retain * reach
        line[j + 3] = reach
    ahead = (enter - coarse_ref[1]) * inv_retain
    ahead = (ahead - coarse_ref[0]) * inv_retain
    line[0] = jnp.where(coefs[0] > 0.0, weight * (ahead + retain * line[1]), 0.0)
    for j in range(-2, 7):
        inside = coefs[min(max(j + 2, 0), 7)] > 0.0
        start = retain * ahead
        line[j + 3] = jnp.where(inside, weight * (start + line[j + 3]), 0.0)
        if j < 6:
            ahead = enter if j == -1 else coarse_ref[j + 2] + start

    smooth = smooth_ref[...]

    for j in range(8):
        v = line[j + 1]
        term = smooth_term(v, coarse_ref[j] + 4.0 * v, coefs[j], line[j], line[j + 2], 2)
        corr[j] = 0.6 * v + apply3(smooth, term)
    for i in range(14):
        field = left_rows[i] if i < 2 else right_rows[i - 12] if i >= 12 else u2_ref[i - 2]
        ua[i] = field + corr[(i - 3) // 2 + 2]

    for source, target, least, most in ((ua, ub, 1, 13), (ub, ua, 2, 12)):
        for i in range(least, most):
            u, (rhs, area) = source[i], row(i + HX - 3)
            term = smooth_term(u, rhs + 4.0 * u, area, source[i - 1], source[i + 1], 1)
            target[i] = 0.6 * u + apply3(smooth, term)
    vert = vert_ref[...]
    for x in range(8):
        i = x + 3
        u = ua[i]
        rhs, area = row(x + HX)
        term = smooth_term(u, rhs, area, ua[i - 1], ua[i + 1], 1)
        rest = term[:, :256] - apply3(vert, u[:, :256])
        for t in range(2):
            here = pl.ds(8 * t + x, K, stride=16)
            pressure_ref[here, :] = u[:, 128 * t : 128 * t + 128]
            residual_ref[here, :] = rest[:, 128 * t : 128 * t + 128]


def local(rhs, areas, stiffness):
    wide, narrow = lax.axis_size("wide"), lax.axis_size("narrow")
    planes = wide // PLANE
    rhs = rhs.reshape(K, 8, 2, 128).transpose(0, 2, 1, 3).reshape(K * 16, 128)
    anywhere = [pl.BlockSpec(memory_space=pltpu.HBM)] * 2
    up, down, own = call(
        pack_x,
        [((HX, KA, 256), f32)] * 2 + [((8, KA, 256), f32)],
        [pltpu.VMEM((K * 16, 128), f32), pltpu.VMEM((8, 256), f32), pltpu.SemaphoreType.DMA((2,))],
        anywhere,
    )(rhs, areas)

    def in_pairs(first, second, axis, count):
        second = lax.ppermute(second, axis, [(i, ((i + 1) ^ 1) - 1) for i in range(1, count - 1)])
        return lax.ppermute(first, axis, [(i, i ^ 1) for i in range(count)]), second

    x_first, x_second = in_pairs(up, down, "wide", wide)
    smooth, vert, retain, weight = call(
        tables,
        [((K, 192), bf16)] * 2 + [((K, 128), f32)] * 2,
        [pltpu.VMEM((K, 128), f32)] * 2,
        [pl.BlockSpec(memory_space=pltpu.SMEM)],
    )(stiffness)
    first, second, left, right = call(
        pack_y, [((KA, 128), f32)] * 2 + [((HX, KA, 256), f32)] * 2, specs=on_vmem(4)
    )(own, x_second, x_first, retain)
    first, second = in_pairs(first, second, "narrow", narrow)
    (u1,) = call(first_main, [((NR, K, 256), f32)], specs=on_vmem(4))(own, left, right, smooth)
    sent, u2, coarse = call(
        before_scan,
        K2_OUTS,
        K2_SCRATCH,
        on_vmem(9),
    )(own, left, right, second, first, u1, smooth, vert, retain)
    in_plane = [[p * PLANE + (s + FIRST_M) % PLANE for s in range(PLANE)] for p in range(planes)]
    over_planes = [[(s + FIRST_Z) % planes * PLANE + m for s in range(planes)] for m in range(PLANE)]

    def exchange(array, groups):
        return lax.all_to_all(array, "wide", 0, 0, tiled=True, axis_index_groups=groups)

    blocks = exchange(sent.reshape(PLANE, 8, LX), in_plane)
    blocks, u2, coarse = lax.optimization_barrier((blocks, u2, coarse))
    deep_first, deep_second = call(pack_deep, [((7, K, 128), f32)] * 2, specs=on_vmem(2))(u2, coarse)
    deep_first, deep_second = in_pairs(deep_first, deep_second, "wide", wide)
    (out,) = call(functools.partial(across_out, planes), [((planes, 8, 256), f32)], specs=on_vmem(2))(blocks, retain)
    others = exchange(out, over_planes)
    (back,) = call(functools.partial(across_in, planes), [((PLANE, 8, LX), f32)], specs=on_vmem(3))(
        blocks, others, retain
    )
    got = exchange(back, in_plane).reshape(K, LX)
    pressure, residual = call(
        after_scan,
        [((K * 16, 128), f32)] * 2,
        K4_SCRATCH,
        on_vmem(14),
    )(got, own, left, right, second, first, u2, coarse, deep_first, deep_second, smooth, vert, retain, weight)
    return tuple(
        out.reshape(K, 2, 8, 128).transpose(0, 2, 1, 3).reshape(K, 8, 256) for out in (pressure, residual)
    )


def solution(mesh):
    placed = (P(None, "wide", "narrow"), P("wide", "narrow"), P())
    return jax.shard_map(
        local,
        mesh=mesh,
        in_specs=placed,
        out_specs=(P(None, "wide", "narrow"), P(None, "wide", "narrow")),
        check_vma=False,
    )
```

```python
import functools

import jax
import jax.numpy as jnp
from jax import lax
from jax.experimental import pallas as pl
from jax.experimental.pallas import tpu as pltpu
from jax.sharding import PartitionSpec as P

K = 64
KA = 72
HX = 2
HY = 8
NR = 8 + 2 * HX
LX = 384
PLANE = 8
FIRST_M = 4
FIRST_Z = 10
f32, bf16 = jnp.float32, jnp.bfloat16
K2_OUTS = [((K, LX), f32), ((10, K, LX), f32), ((2, K, LX), f32)]
K2_SCRATCH = [pltpu.VMEM(s, f32) for s in ((NR, KA, 128), (NR, K, LX), (4, K, LX), (NR, K, 128))]
K4_SCRATCH = [
    pltpu.VMEM(s, f32)
    for s in ((NR, KA, 128), (8, K, LX), (10, K, LX), (8, K, LX), (14, K, LX), (14, K, LX))
]
LIMIT = 16 * 1024 * 1024


def call(kernel, outs, scratch=(), specs=None):
    vmem = pl.BlockSpec(memory_space=pltpu.VMEM)
    return pl.pallas_call(
        kernel,
        out_shape=[jax.ShapeDtypeStruct(s, d) for s, d in outs],
        in_specs=specs,
        out_specs=[vmem] * len(outs),
        scratch_shapes=list(scratch),
        compiler_params=pltpu.CompilerParams(vmem_limit_bytes=LIMIT),
    )


def on_vmem(n):
    return [pl.BlockSpec(memory_space=pltpu.VMEM)] * n


def lanes(shape):
    return lax.broadcasted_iota(jnp.int32, shape, len(shape) - 1)


def wide3(table):
    return jnp.concatenate([table] * (LX // 128), axis=1)


def apply3(cat, x):
    high = x.astype(bf16)
    low = (x - high.astype(f32)).astype(bf16)
    return jnp.dot(cat, jnp.concatenate([high, high, low], axis=0), preferred_element_type=f32)


def select(x, picks):
    high = x.astype(bf16)
    rest = x - high.astype(f32)
    middle = rest.astype(bf16)
    low = (rest - middle.astype(f32)).astype(bf16)
    rows = x.shape[0]
    parts = jnp.dot(jnp.concatenate([high, middle, low], axis=0), picks.astype(bf16), preferred_element_type=f32)
    return parts[:rows] + (parts[rows : 2 * rows] + parts[2 * rows :])


def split3(matrix):
    high = matrix.astype(bf16)
    low = (matrix - high.astype(f32)).astype(bf16)
    return jnp.concatenate([high, low, high], axis=1)


def pack_x(rhs_hbm, areas_hbm, first_ref, second_ref, own_ref, rhs, areas, sems):
    copies = [
        pltpu.make_async_copy(rhs_hbm, rhs, sems.at[0]),
        pltpu.make_async_copy(areas_hbm, areas, sems.at[1]),
    ]
    for copy in copies:
        copy.start()
    for copy in copies:
        copy.wait()
    first = lax.broadcasted_iota(jnp.int32, (KA - K, 256), 0) == 0

    def area(x, beyond):
        return jnp.where(first, areas[x : x + 1, :], areas[beyond : beyond + 1, :])

    for x in range(8):
        for t in range(2):
            own_ref[x, :K, 128 * t : 128 * t + 128] = rhs[pl.ds(8 * t + x, K, stride=16), :]
        own_ref[x, K:, :] = area(x, x)
    even = lax.rem(lax.axis_index("wide"), 2) == 0
    for x in range(HX):
        up, down = own_ref[8 - HX + x, :K, :], own_ref[x, :K, :]
        up_area, down_area = area(8 - HX + x, 8 - 2 * HX + x), area(x, x + HX)
        first_ref[x, :K, :] = jnp.where(even, up, down)
        first_ref[x, K:, :] = jnp.where(even, up_area, down_area)
        second_ref[x, :K, :] = jnp.where(even, down, up)
        second_ref[x, K:, :] = jnp.where(even, down_area, up_area)


def tables(stiff_ref, smooth_ref, vert_ref, retain_ref, weight_ref, lead, trail):
    scale = 7.5
    row = lax.broadcasted_iota(jnp.int32, (K, 128), 0)
    col = lax.broadcasted_iota(jnp.int32, (K, 128), 1)
    lane = lanes((1, 128))
    one = jnp.ones((1, 128), f32)
    zero = jnp.zeros((1, 128), f32)
    before, now, lead_row = zero, one, zero
    after, later, trail_row = zero, one, zero
    for k in range(K):
        lead[pl.ds(k, 1), :] = now
        lead_row = jnp.where(lane == k, now, lead_row)
        now, before = (stiff_ref[k] + 8.0) * (1.0 / scale) * now - (4.0 / scale**2) * before, now
        at = K - 1 - k
        trail[pl.ds(at, 1), :] = later
        trail_row = jnp.where(lane == at, later, trail_row)
        later, after = (stiff_ref[at] + 8.0) * (1.0 / scale) * later - (4.0 / scale**2) * after, later
    gap = jnp.abs(row - col)
    decay = jnp.ones((K, 128), f32)
    for b in range(6):
        decay = decay * jnp.where((gap >> b) & 1 == 1, (2.0 / scale) ** (1 << b), 1.0)
    upper = lead[...] * trail_row
    lower = lead_row * trail[...]
    inverse = decay * jnp.where(row <= col, upper, lower) / (scale * now)
    smooth_ref[...] = split3((0.4 * inverse)[:, :K])
    stiff_row = zero
    for k in range(K):
        stiff_row = jnp.where(lane == k, stiff_ref[k], stiff_row)
    diagonal = jnp.where(row == col, stiff_row, 0.0)
    stiff = jnp.broadcast_to(jnp.sum(diagonal, axis=1, keepdims=True), (K, 128))
    vert = jnp.where(row == col, stiff + 4.0, jnp.where(gap == 1, -2.0, 0.0))
    vert_ref[...] = split3(vert[:, :K])
    keep = jnp.sqrt(stiff + 0.25 * stiff * stiff) - 0.5 * stiff
    retain_ref[...] = 1.0 - keep
    weight_ref[...] = keep / (2.0 - keep)


def ext_row(own_ref, left_ref, right_ref, r):
    if r < HX:
        return left_ref[r]
    if r >= HX + 8:
        return right_ref[r - HX - 8]
    return own_ref[r - HX]


def whole_row(own_ref, left_ref, right_ref, tails_ref, r, levels=K):
    main = ext_row(own_ref, left_ref, right_ref, r)
    tail = tails_ref[r]
    at = slice(levels, levels + 1)
    return (
        jnp.concatenate([main[:K], tail[:K]], axis=1),
        jnp.concatenate([main[at], tail[at]], axis=1),
    )


def pack_y(own_ref, x_second_ref, x_first_ref, _, first_ref, second_ref, left_ref, right_ref):
    even = lax.rem(lax.axis_index("wide"), 2) == 0
    left_ref[...] = jnp.where(even, x_second_ref[...], x_first_ref[...])
    right_ref[...] = jnp.where(even, x_first_ref[...], x_second_ref[...])
    lane = lanes((KA, 128))
    low = high = jnp.zeros((KA, 128), f32)
    for r in range(NR):
        row = ext_row(own_ref, left_ref, right_ref, r)
        o = HY * r
        here = (lane >= o) & (lane < o + HY)
        low = jnp.where(here, pltpu.roll(row[:, :128], o, 1), low)
        high = jnp.where(here, pltpu.roll(row[:, 128:], o + HY, 1), high)
    even = lax.rem(lax.axis_index("narrow"), 2) == 0
    first_ref[...] = jnp.where(even, high, low)
    second_ref[...] = jnp.where(even, low, high)


def first_main(own_ref, left_ref, right_ref, smooth_ref, u1_ref):
    smooth = smooth_ref[...]
    for r in range(NR):
        u1_ref[r] = apply3(smooth, ext_row(own_ref, left_ref, right_ref, r)[:K])


def smooth_term(u, rhs, area, above, below, step, more=0.0):
    beside = above + below + pltpu.roll(u, step, 1) + pltpu.roll(u, LX - step, 1)
    return rhs + ((more - 4.0 * area) * u + area * beside)


def pair_sum(v):
    even = lanes(v.shape) % 2 == 0
    return v + jnp.where(even, pltpu.roll(v, LX - 1, 1), pltpu.roll(v, 1, 1))


def y_sides(first_ref, second_ref):
    even = lax.rem(lax.axis_index("narrow"), 2) == 0
    first, second = first_ref[...], second_ref[...]
    return jnp.where(even, first, second), jnp.where(even, second, first)


def beyond(right, left, r):
    lane = lanes(right.shape)
    right = pltpu.roll(right, (128 - HY * r) % 128, 1)
    left = pltpu.roll(left, 128 - HY - HY * r, 1)
    return jnp.where(lane < HY, right, jnp.where(lane >= 128 - HY, left, 0.0))


def pack_deep(u2_ref, both_ref, first_ref, second_ref):
    lane = lanes((K, 128))
    even = lax.rem(lax.axis_index("wide"), 2) == 0
    tails = [jnp.zeros((K, 128), f32)] * 2
    for i in range(3):
        if i < 2:
            sides = u2_ref[6 + i], u2_ref[2 + i]
        else:
            sides = both_ref[1], both_ref[0]
        here = (lane >= 16 * i) & (lane < 16 * i + 16)
        rows = jnp.where(even, sides[0], sides[1]), jnp.where(even, sides[1], sides[0])
        for n, ref in enumerate((first_ref, second_ref)):
            ref[2 * i] = rows[n][:, :128]
            ref[2 * i + 1] = rows[n][:, 128:256]
            tails[n] = jnp.where(here, pltpu.roll(rows[n][:, 256:], HY + 16 * i, 1), tails[n])
    first_ref[6] = tails[0]
    second_ref[6] = tails[1]


def unpack_deep(got):
    lane = lanes((K, 128))
    edge = (lane < HY) | (lane >= 128 - HY)
    rows = []
    for i in range(3):
        tail = jnp.where(edge, pltpu.roll(got(6), 128 - HY - 16 * i, 1), 0.0)
        rows.append(jnp.concatenate([got(2 * i), got(2 * i + 1), tail], axis=1))
    return rows, unfold(rows.pop())


def unfold(both):
    even = lanes((K, LX)) % 2 == 0
    first = jnp.where(even, both, pltpu.roll(both, 1, 1))
    second = jnp.where(even, pltpu.roll(both, LX - 1, 1), both)
    return first, second


def before_scan(
    own_ref, left_ref, right_ref, second_ref, first_ref, u1_ref, smooth_ref, vert_ref, retain_ref,
    sent_ref, u2_ref, both_ref, tails_ref, fine, coarse_ref, u1,
):
    smooth = smooth_ref[...]
    low, high = y_sides(first_ref, second_ref)
    tails = apply3(smooth, jnp.concatenate([low[:K], high[:K]], axis=1))

    for r in range(NR):
        tails_ref[r] = beyond(low, high, r)
        u1[r] = beyond(tails[:, :128], tails[:, 128:], r)

    def row(r):
        return whole_row(own_ref, left_ref, right_ref, tails_ref, r)

    def first(r):
        return jnp.concatenate([u1_ref[r], u1[r]], axis=1)

    for r in range(1, NR - 1):
        u, (rhs, area) = first(r), row(r)
        term = smooth_term(u, rhs, area, first(r - 1), first(r + 1), 1, 4.0)
        fine[r] = 0.6 * u + apply3(smooth, term)
    vert = vert_ref[...]
    for j in range(4):
        total, field = 0.0, 0.0
        for at in (2 * j + HX, 2 * j + HX + 1):
            u, (rhs, area) = fine[at], row(at)
            total += smooth_term(u, rhs, area, fine[at - 1], fine[at + 1], 1)
            field += u
        coarse_ref[j] = 0.25 * (pair_sum(total) - apply3(vert, pair_sum(field)))
    for x in range(10):
        u2_ref[x] = fine[x + 1]
    parity = lanes((K, LX)) % 2 == 0
    for j in range(2):
        both_ref[j] = jnp.where(parity, coarse_ref[2 * j], coarse_ref[2 * j + 1])
    retain = wide3(retain_ref[...])
    ahead = coarse_ref[0]
    back = coarse_ref[3]
    for j in range(1, 4):
        ahead = retain * ahead + coarse_ref[j]
        back = retain * back + coarse_ref[3 - j]
    fine_lane = lax.broadcasted_iota(jnp.int32, (LX, 256), 0)
    coarse_lane = lax.broadcasted_iota(jnp.int32, (LX, 256), 1)
    pick = jnp.where(fine_lane == 2 * coarse_lane, 1.0, 0.0)
    both = select(jnp.concatenate([ahead, back], axis=0), pick)
    sent_ref[:, :128] = both[:K, :128]
    sent_ref[:, 128:256] = both[K:, :128]
    sent_ref[:, 256:] = both[:K, 128:] + pltpu.roll(both[K:, 128:], 64, 1)


def power(x, n):
    out = None
    while n:
        if n & 1:
            out = x if out is None else out * x
        x = x * x
        n >>= 1
    return out


def my_retain(retain_ref):
    at = lax.rem(lax.axis_index("wide") + PLANE - FIRST_M, PLANE)
    return retain_ref[pl.ds(pl.multiple_of(at * 8, 8), 8), :]


def beyond_here(planes, here, retain):
    left, step = planes - 1 - here, power(retain, 64)
    out = jnp.ones_like(retain)
    for b in range((planes - 1).bit_length()):
        out = jnp.where((left >> b) & 1 == 1, out * step, out)
        step = step * step
    return out


def slot_m(m):
    return (m - FIRST_M) % PLANE


def slot_z(q, planes):
    return (q - FIRST_Z) % planes


def plane_ends(blocks, retain):
    four = power(retain, 4)
    ends = []
    for order, part in ((range(PLANE), 0), (reversed(range(PLANE)), 1)):
        main, tail = 0.0, 0.0
        for m in order:
            main = four * main + blocks[slot_m(m), :, 128 * part : 128 * part + 128]
            tail = four * tail + blocks[slot_m(m), :, 256:]
        ends += [main, tail if part == 0 else pltpu.roll(tail, 64, 1)]
    return ends


def across_out(planes, blocks_ref, retain_ref, out_ref):
    retain = my_retain(retain_ref)
    here = lax.div(lax.axis_index("wide"), PLANE)
    ahead, ahead_tail, back, back_tail = plane_ends(blocks_ref, retain)
    reflect = power(retain, 33) * beyond_here(planes, here, retain)
    back = back - reflect * ahead
    back_tail = back_tail - reflect * ahead_tail
    for q in range(planes):
        out_ref[slot_z(q, planes), :, :128] = jnp.where(q > here, ahead, back)
        out_ref[slot_z(q, planes), :, 128:] = jnp.where(q > here, ahead_tail, back_tail)


def across_in(planes, blocks_ref, others_ref, retain_ref, out_ref):
    retain = my_retain(retain_ref)
    here = lax.div(lax.axis_index("wide"), PLANE)
    ahead, ahead_tail, _, _ = plane_ends(blocks_ref, retain)
    four, plane = power(retain, 4), power(retain, 32)
    reflect = retain * beyond_here(planes, here, retain)
    enter, leave = [0.0, 0.0], [0.0, 0.0]
    for q in range(planes):
        back = planes - 1 - q
        for part in range(2):
            at = slice(128 * part, 128 * part + 128)
            enter[part] = jnp.where(q < here, plane * enter[part] + others_ref[slot_z(q, planes), :, at], enter[part])
            leave[part] = jnp.where(back > here, plane * leave[part] + others_ref[slot_z(back, planes), :, at], leave[part])
    leave[0] = leave[0] - reflect * (ahead + plane * enter[0])
    leave[1] = leave[1] - reflect * (ahead_tail + plane * enter[1])
    left = lanes((8, 128)) < 64
    leave[1] = pltpu.roll(leave[1], 64, 1)
    tails = []
    for m in range(PLANE):
        out_ref[slot_m(m), :, :128] = enter[0]
        tails.append(enter[1])
        enter[0] = four * enter[0] + blocks_ref[slot_m(m), :, :128]
        enter[1] = four * enter[1] + blocks_ref[slot_m(m), :, 256:]
    for m in reversed(range(PLANE)):
        out_ref[slot_m(m), :, 128:256] = leave[0]
        out_ref[slot_m(m), :, 256:] = jnp.where(left, tails[m], leave[1])
        leave[0] = four * leave[0] + blocks_ref[slot_m(m), :, 128:256]
        leave[1] = four * leave[1] + blocks_ref[slot_m(m), :, 256:]


def after_scan(
    got_ref, own_ref, left_ref, right_ref, y_second_ref, y_first_ref, u2_ref, both_ref, deep_first_ref, deep_second_ref, smooth_ref, vert_ref, retain_ref, weight_ref,
    pressure_ref, residual_ref, tails_ref, coarse_ref, line, corr, ua, ub,
):
    even = lax.rem(lax.axis_index("wide"), 2) == 0
    left_rows, left_coarse = unpack_deep(lambda i: jnp.where(even, deep_second_ref[i], deep_first_ref[i]))
    right_rows, right_coarse = unpack_deep(lambda i: jnp.where(even, deep_first_ref[i], deep_second_ref[i]))
    for j in range(2):
        coarse_ref[j] = left_coarse[j]
        coarse_ref[6 + j] = right_coarse[j]
    for j in range(2):
        coarse_ref[2 + 2 * j], coarse_ref[3 + 2 * j] = unfold(both_ref[j])
    low, high = y_sides(y_first_ref, y_second_ref)
    for r in range(NR):
        tails_ref[r] = beyond(low, high, r)
    retain, weight = wide3(retain_ref[...]), wide3(weight_ref[...])
    inv_retain = 1.0 / retain
    coarse_lane = lax.broadcasted_iota(jnp.int32, (256, LX), 0)
    fine_lane = lax.broadcasted_iota(jnp.int32, (256, LX), 1)
    spread = jnp.where(fine_lane // 2 == coarse_lane, 1.0, 0.0)
    keep_left = lanes((K, 128)) < 64
    tail = got_ref[:, 256:]
    both = jnp.concatenate(
        [
            jnp.concatenate([got_ref[:, :128], jnp.where(keep_left, tail, 0.0)], axis=1),
            jnp.concatenate([got_ref[:, 128:256], jnp.where(keep_left, pltpu.roll(tail, 64, 1), 0.0)], axis=1),
        ],
        axis=0,
    )
    both = select(both, spread)

    def row(r, levels=K):
        return whole_row(own_ref, left_ref, right_ref, tails_ref, r, levels)

    def coef(j):
        if j == 0:
            pair = row(0, K + 1)[1] + row(1, K + 1)[1]
        elif j == 7:
            pair = row(NR - 2, K + 1)[1] + row(NR - 1, K + 1)[1]
        else:
            pair = row(2 * j + HX - 4)[1] + row(2 * j + HX - 3)[1]
        return 0.0625 * pair_sum(pair)

    coefs = [coef(j) for j in range(8)]
    enter, leave = both[:K], both[K:]
    reach = leave
    for j in (4, 5):
        reach = (reach - coarse_ref[j + 2]) * inv_retain
        line[j + 1 + 3] = reach
    reach = leave
    line[4 + 3] = reach
    for j in (3, 2, 1, 0, -1, -2):
        reach = coarse_ref[j + 2] + retain * reach
        line[j + 3] = reach
    ahead = (enter - coarse_ref[1]) * inv_retain
    ahead = (ahead - coarse_ref[0]) * inv_retain
    line[0] = jnp.where(coefs[0] > 0.0, weight * (ahead + retain * line[1]), 0.0)
    for j in range(-2, 7):
        inside = coefs[min(max(j + 2, 0), 7)] > 0.0
        start = retain * ahead
        line[j + 3] = jnp.where(inside, weight * (start + line[j + 3]), 0.0)
        if j < 6:
            ahead = enter if j == -1 else coarse_ref[j + 2] + start

    smooth = smooth_ref[...]

    for j in range(8):
        v = line[j + 1]
        term = smooth_term(v, coarse_ref[j], coefs[j], line[j], line[j + 2], 2, 4.0)
        corr[j] = 0.6 * v + apply3(smooth, term)
    for i in range(14):
        field = left_rows[i] if i < 2 else right_rows[i - 12] if i >= 12 else u2_ref[i - 2]
        ua[i] = field + corr[(i - 3) // 2 + 2]

    for source, target, least, most in ((ua, ub, 1, 13), (ub, ua, 2, 12)):
        for i in range(least, most):
            u, (rhs, area) = source[i], row(i + HX - 3)
            term = smooth_term(u, rhs, area, source[i - 1], source[i + 1], 1, 4.0)
            target[i] = 0.6 * u + apply3(smooth, term)
    vert = vert_ref[...]
    for x in range(8):
        i = x + 3
        u = ua[i]
        rhs, area = row(x + HX)
        term = smooth_term(u, rhs, area, ua[i - 1], ua[i + 1], 1)
        rest = term[:, :256] - apply3(vert, u[:, :256])
        for t in range(2):
            here = pl.ds(8 * t + x, K, stride=16)
            pressure_ref[here, :] = u[:, 128 * t : 128 * t + 128]
            residual_ref[here, :] = rest[:, 128 * t : 128 * t + 128]


def local(rhs, areas, stiffness):
    wide, narrow = lax.axis_size("wide"), lax.axis_size("narrow")
    planes = wide // PLANE
    rhs = rhs.reshape(K, 8, 2, 128).transpose(0, 2, 1, 3).reshape(K * 16, 128)
    up, down, own = call(
        pack_x,
        [((HX, KA, 256), f32)] * 2 + [((8, KA, 256), f32)],
        [pltpu.VMEM((K * 16, 128), f32), pltpu.VMEM((8, 256), f32), pltpu.SemaphoreType.DMA((2,))],
        [pl.BlockSpec(memory_space=pltpu.HBM)] * 2,
    )(*(pltpu.with_memory_space_constraint(x, pltpu.HBM) for x in (rhs, areas)))

    def in_pairs(first, second, axis, count):
        second = lax.ppermute(second, axis, [(i, ((i + 1) ^ 1) - 1) for i in range(1, count - 1)])
        return lax.ppermute(first, axis, [(i, i ^ 1) for i in range(count)]), second

    x_first, x_second = in_pairs(up, down, "wide", wide)
    smooth, vert, retain, weight = call(
        tables,
        [((K, 192), bf16)] * 2 + [((K, 128), f32)] * 2,
        [pltpu.VMEM((K, 128), f32)] * 2,
        [pl.BlockSpec(memory_space=pltpu.SMEM)],
    )(stiffness)
    first, second, left, right = call(
        pack_y, [((KA, 128), f32)] * 2 + [((HX, KA, 256), f32)] * 2, specs=on_vmem(4)
    )(own, x_second, x_first, retain)
    first, second = in_pairs(first, second, "narrow", narrow)
    (u1,) = call(first_main, [((NR, K, 256), f32)], specs=on_vmem(4))(own, left, right, smooth)
    sent, u2, coarse = call(
        before_scan,
        K2_OUTS,
        K2_SCRATCH,
        on_vmem(9),
    )(own, left, right, second, first, u1, smooth, vert, retain)
    in_plane = [[p * PLANE + (s + FIRST_M) % PLANE for s in range(PLANE)] for p in range(planes)]
    over_planes = [[(s + FIRST_Z) % planes * PLANE + m for s in range(planes)] for m in range(PLANE)]

    def exchange(array, groups):
        return lax.all_to_all(array, "wide", 0, 0, tiled=True, axis_index_groups=groups)

    blocks = exchange(sent.reshape(PLANE, 8, LX), in_plane)
    blocks, u2, coarse = lax.optimization_barrier((blocks, u2, coarse))
    deep_first, deep_second = call(pack_deep, [((7, K, 128), f32)] * 2, specs=on_vmem(2))(u2, coarse)
    deep_first, deep_second = in_pairs(deep_first, deep_second, "wide", wide)
    (out,) = call(functools.partial(across_out, planes), [((planes, 8, 256), f32)], specs=on_vmem(2))(blocks, retain)
    others = exchange(out, over_planes)
    (back,) = call(functools.partial(across_in, planes), [((PLANE, 8, LX), f32)], specs=on_vmem(3))(
        blocks, others, retain
    )
    got = exchange(back, in_plane).reshape(K, LX)
    pressure, residual = call(
        after_scan,
        [((K * 16, 128), f32)] * 2,
        K4_SCRATCH,
        on_vmem(14),
    )(got, own, left, right, second, first, u2, coarse, deep_first, deep_second, smooth, vert, retain, weight)
    return tuple(
        out.reshape(K, 2, 8, 128).transpose(0, 2, 1, 3).reshape(K, 8, 256) for out in (pressure, residual)
    )


def solution(mesh):
    placed = (P(None, "wide", "narrow"), P("wide", "narrow"), P())
    return jax.shard_map(
        local,
        mesh=mesh,
        in_specs=placed,
        out_specs=(P(None, "wide", "narrow"), P(None, "wide", "narrow")),
        check_vma=False,
    )
```

```python
import functools

import jax
import jax.numpy as jnp
from jax import lax
from jax.experimental import pallas as pl
from jax.experimental.pallas import tpu as pltpu
from jax.sharding import PartitionSpec as P

K = 64
KA = 72
HX = 2
HY = 8
NR = 8 + 2 * HX
LX = 384
PLANE = 8
FIRST_M = 4
FIRST_Z = 10
f32, bf16 = jnp.float32, jnp.bfloat16
K2_OUTS = [((K, LX), f32), ((10, K, LX), f32), ((2, K, LX), f32)]
K2_SCRATCH = [pltpu.VMEM(s, f32) for s in ((NR, KA, 128), (NR, K, LX), (4, K, LX), (NR, K, 128))]
K4_SCRATCH = [
    pltpu.VMEM(s, f32)
    for s in ((NR, KA, 128), (8, K, LX), (10, K, LX), (8, K, LX), (14, K, LX), (14, K, LX))
]
LIMIT = 16 * 1024 * 1024


def call(kernel, outs, scratch=(), specs=None):
    vmem = pl.BlockSpec(memory_space=pltpu.VMEM)
    return pl.pallas_call(
        kernel,
        out_shape=[jax.ShapeDtypeStruct(s, d) for s, d in outs],
        in_specs=specs,
        out_specs=[vmem] * len(outs),
        scratch_shapes=list(scratch),
        compiler_params=pltpu.CompilerParams(vmem_limit_bytes=LIMIT),
    )


def on_vmem(n):
    return [pl.BlockSpec(memory_space=pltpu.VMEM)] * n


def lanes(shape):
    return lax.broadcasted_iota(jnp.int32, shape, len(shape) - 1)


def wide3(table):
    return jnp.concatenate([table] * (LX // 128), axis=1)


def apply3(cat, x):
    high = x.astype(bf16)
    low = (x - high.astype(f32)).astype(bf16)
    return jnp.dot(cat, jnp.concatenate([high, high, low], axis=0), preferred_element_type=f32)


def select(x, picks):
    high = x.astype(bf16)
    rest = x - high.astype(f32)
    middle = rest.astype(bf16)
    low = (rest - middle.astype(f32)).astype(bf16)
    rows = x.shape[0]
    parts = jnp.dot(jnp.concatenate([high, middle, low], axis=0), picks.astype(bf16), preferred_element_type=f32)
    return parts[:rows] + (parts[rows : 2 * rows] + parts[2 * rows :])


def split3(matrix):
    high = matrix.astype(bf16)
    low = (matrix - high.astype(f32)).astype(bf16)
    return jnp.concatenate([high, low, high], axis=1)


def pack_x(rhs_hbm, areas_hbm, first_ref, second_ref, own_ref, rhs, areas, sems):
    copies = [
        pltpu.make_async_copy(rhs_hbm, rhs, sems.at[0]),
        pltpu.make_async_copy(areas_hbm, areas, sems.at[1]),
    ]
    for copy in copies:
        copy.start()
    for copy in copies:
        copy.wait()
    first = lax.broadcasted_iota(jnp.int32, (KA - K, 256), 0) == 0

    def area(x, beyond):
        return jnp.where(first, areas[x : x + 1, :], areas[beyond : beyond + 1, :])

    for x in range(8):
        for t in range(2):
            own_ref[x, :K, 128 * t : 128 * t + 128] = rhs[pl.ds(8 * t + x, K, stride=16), :]
        own_ref[x, K:, :] = area(x, x)
    even = lax.rem(lax.axis_index("wide"), 2) == 0
    for x in range(HX):
        up, down = own_ref[8 - HX + x, :K, :], own_ref[x, :K, :]
        up_area, down_area = area(8 - HX + x, 8 - 2 * HX + x), area(x, x + HX)
        first_ref[x, :K, :] = jnp.where(even, up, down)
        first_ref[x, K:, :] = jnp.where(even, up_area, down_area)
        second_ref[x, :K, :] = jnp.where(even, down, up)
        second_ref[x, K:, :] = jnp.where(even, down_area, up_area)


def tables(stiff_ref, smooth_ref, vert_ref, retain_ref, weight_ref, lead, trail):
    scale = 7.5
    row = lax.broadcasted_iota(jnp.int32, (K, 128), 0)
    col = lax.broadcasted_iota(jnp.int32, (K, 128), 1)
    lane = lanes((1, 128))
    one = jnp.ones((1, 128), f32)
    zero = jnp.zeros((1, 128), f32)
    before, now, lead_row = zero, one, zero
    after, later, trail_row = zero, one, zero
    for k in range(K):
        lead[pl.ds(k, 1), :] = now
        lead_row = jnp.where(lane == k, now, lead_row)
        now, before = (stiff_ref[k] + 8.0) * (1.0 / scale) * now - (4.0 / scale**2) * before, now
        at = K - 1 - k
        trail[pl.ds(at, 1), :] = later
        trail_row = jnp.where(lane == at, later, trail_row)
        later, after = (stiff_ref[at] + 8.0) * (1.0 / scale) * later - (4.0 / scale**2) * after, later
    gap = jnp.abs(row - col)
    decay = jnp.ones((K, 128), f32)
    for b in range(6):
        decay = decay * jnp.where((gap >> b) & 1 == 1, (2.0 / scale) ** (1 << b), 1.0)
    upper = lead[...] * trail_row
    lower = lead_row * trail[...]
    inverse = decay * jnp.where(row <= col, upper, lower) / (scale * now)
    smooth_ref[...] = split3((0.4 * inverse)[:, :K])
    stiff_row = zero
    for k in range(K):
        stiff_row = jnp.where(lane == k, stiff_ref[k], stiff_row)
    diagonal = jnp.where(row == col, stiff_row, 0.0)
    stiff = jnp.broadcast_to(jnp.sum(diagonal, axis=1, keepdims=True), (K, 128))
    vert = jnp.where(row == col, stiff + 4.0, jnp.where(gap == 1, -2.0, 0.0))
    vert_ref[...] = split3(vert[:, :K])
    keep = jnp.sqrt(stiff + 0.25 * stiff * stiff) - 0.5 * stiff
    retain_ref[...] = 1.0 - keep
    weight_ref[...] = keep / (2.0 - keep)


def ext_row(own_ref, left_ref, right_ref, r):
    if r < HX:
        return left_ref[r]
    if r >= HX + 8:
        return right_ref[r - HX - 8]
    return own_ref[r - HX]


def whole_row(own_ref, left_ref, right_ref, tails_ref, r, levels=K):
    main = ext_row(own_ref, left_ref, right_ref, r)
    tail = tails_ref[r]
    at = slice(levels, levels + 1)
    return (
        jnp.concatenate([main[:K], tail[:K]], axis=1),
        jnp.concatenate([main[at], tail[at]], axis=1),
    )


def pack_y(own_ref, x_first_ref, x_second_ref, _, first_ref, second_ref, left_ref, right_ref):
    even = lax.rem(lax.axis_index("wide"), 2) == 0
    left_ref[...] = jnp.where(even, x_second_ref[...], x_first_ref[...])
    right_ref[...] = jnp.where(even, x_first_ref[...], x_second_ref[...])
    lane = lanes((KA, 128))
    low = high = jnp.zeros((KA, 128), f32)
    for r in range(NR):
        row = ext_row(own_ref, left_ref, right_ref, r)
        o = HY * r
        here = (lane >= o) & (lane < o + HY)
        low = jnp.where(here, pltpu.roll(row[:, :128], o, 1), low)
        high = jnp.where(here, pltpu.roll(row[:, 128:], o + HY, 1), high)
    even = lax.rem(lax.axis_index("narrow"), 2) == 0
    first_ref[...] = jnp.where(even, high, low)
    second_ref[...] = jnp.where(even, low, high)


def first_main(own_ref, left_ref, right_ref, smooth_ref, u1_ref):
    smooth = smooth_ref[...]
    for r in range(NR):
        u1_ref[r] = apply3(smooth, ext_row(own_ref, left_ref, right_ref, r)[:K])


def smooth_term(u, rhs, area, above, below, step, more=0.0):
    beside = above + below + pltpu.roll(u, step, 1) + pltpu.roll(u, LX - step, 1)
    return rhs + ((more - 4.0 * area) * u + area * beside)


def pair_sum(v):
    even = lanes(v.shape) % 2 == 0
    return v + jnp.where(even, pltpu.roll(v, LX - 1, 1), pltpu.roll(v, 1, 1))


def y_sides(first_ref, second_ref):
    even = lax.rem(lax.axis_index("narrow"), 2) == 0
    first, second = first_ref[...], second_ref[...]
    return jnp.where(even, first, second), jnp.where(even, second, first)


def beyond(right, left, r):
    lane = lanes(right.shape)
    right = pltpu.roll(right, (128 - HY * r) % 128, 1)
    left = pltpu.roll(left, 128 - HY - HY * r, 1)
    return jnp.where(lane < HY, right, jnp.where(lane >= 128 - HY, left, 0.0))


def pack_deep(u2_ref, both_ref, first_ref, second_ref):
    lane = lanes((K, 128))
    even = lax.rem(lax.axis_index("wide"), 2) == 0
    tails = [jnp.zeros((K, 128), f32)] * 2
    for i in range(3):
        if i < 2:
            sides = u2_ref[6 + i], u2_ref[2 + i]
        else:
            sides = both_ref[1], both_ref[0]
        here = (lane >= 16 * i) & (lane < 16 * i + 16)
        rows = jnp.where(even, sides[0], sides[1]), jnp.where(even, sides[1], sides[0])
        for n, ref in enumerate((first_ref, second_ref)):
            ref[2 * i] = rows[n][:, :128]
            ref[2 * i + 1] = rows[n][:, 128:256]
            tails[n] = jnp.where(here, pltpu.roll(rows[n][:, 256:], HY + 16 * i, 1), tails[n])
    first_ref[6] = tails[0]
    second_ref[6] = tails[1]


def unpack_deep(got):
    lane = lanes((K, 128))
    edge = (lane < HY) | (lane >= 128 - HY)
    rows = []
    for i in range(3):
        tail = jnp.where(edge, pltpu.roll(got(6), 128 - HY - 16 * i, 1), 0.0)
        rows.append(jnp.concatenate([got(2 * i), got(2 * i + 1), tail], axis=1))
    return rows, unfold(rows.pop())


def unfold(both):
    even = lanes((K, LX)) % 2 == 0
    first = jnp.where(even, both, pltpu.roll(both, 1, 1))
    second = jnp.where(even, pltpu.roll(both, LX - 1, 1), both)
    return first, second


def before_scan(
    own_ref, left_ref, right_ref, second_ref, first_ref, u1_ref, smooth_ref, vert_ref, retain_ref,
    sent_ref, u2_ref, both_ref, tails_ref, fine, coarse_ref, u1,
):
    smooth = smooth_ref[...]
    low, high = y_sides(first_ref, second_ref)
    tails = apply3(smooth, jnp.concatenate([low[:K], high[:K]], axis=1))

    for r in range(NR):
        tails_ref[r] = beyond(low, high, r)
        u1[r] = beyond(tails[:, :128], tails[:, 128:], r)

    def row(r):
        return whole_row(own_ref, left_ref, right_ref, tails_ref, r)

    def first(r):
        return jnp.concatenate([u1_ref[r], u1[r]], axis=1)

    for r in range(1, NR - 1):
        u, (rhs, area) = first(r), row(r)
        term = smooth_term(u, rhs, area, first(r - 1), first(r + 1), 1, 4.0)
        fine[r] = 0.6 * u + apply3(smooth, term)
    vert = vert_ref[...]
    for j in range(4):
        total, field = 0.0, 0.0
        for at in (2 * j + HX, 2 * j + HX + 1):
            u, (rhs, area) = fine[at], row(at)
            total += smooth_term(u, rhs, area, fine[at - 1], fine[at + 1], 1)
            field += u
        coarse_ref[j] = 0.25 * (pair_sum(total) - apply3(vert, pair_sum(field)))
    for x in range(10):
        u2_ref[x] = fine[x + 1]
    parity = lanes((K, LX)) % 2 == 0
    for j in range(2):
        both_ref[j] = jnp.where(parity, coarse_ref[2 * j], coarse_ref[2 * j + 1])
    retain = wide3(retain_ref[...])
    ahead = coarse_ref[0]
    back = coarse_ref[3]
    for j in range(1, 4):
        ahead = retain * ahead + coarse_ref[j]
        back = retain * back + coarse_ref[3 - j]
    fine_lane = lax.broadcasted_iota(jnp.int32, (LX, 256), 0)
    coarse_lane = lax.broadcasted_iota(jnp.int32, (LX, 256), 1)
    pick = jnp.where(fine_lane == 2 * coarse_lane, 1.0, 0.0)
    both = select(jnp.concatenate([ahead, back], axis=0), pick)
    sent_ref[:, :128] = both[:K, :128]
    sent_ref[:, 128:256] = both[K:, :128]
    sent_ref[:, 256:] = both[:K, 128:] + pltpu.roll(both[K:, 128:], 64, 1)


def power(x, n):
    out = None
    while n:
        if n & 1:
            out = x if out is None else out * x
        x = x * x
        n >>= 1
    return out


def my_retain(retain_ref):
    at = lax.rem(lax.axis_index("wide") + PLANE - FIRST_M, PLANE)
    return retain_ref[pl.ds(pl.multiple_of(at * 8, 8), 8), :]


def beyond_here(planes, here, retain):
    left, step = planes - 1 - here, power(retain, 64)
    out = jnp.ones_like(retain)
    for b in range((planes - 1).bit_length()):
        out = jnp.where((left >> b) & 1 == 1, out * step, out)
        step = step * step
    return out


def slot_m(m):
    return (m - FIRST_M) % PLANE


def slot_z(q, planes):
    return (q - FIRST_Z) % planes


def plane_ends(blocks, retain):
    four = power(retain, 4)
    ends = []
    for order, part in ((range(PLANE), 0), (reversed(range(PLANE)), 1)):
        main, tail = 0.0, 0.0
        for m in order:
            main = four * main + blocks[slot_m(m), :, 128 * part : 128 * part + 128]
            tail = four * tail + blocks[slot_m(m), :, 256:]
        ends += [main, tail if part == 0 else pltpu.roll(tail, 64, 1)]
    return ends


def across_out(planes, blocks_ref, retain_ref, out_ref):
    retain = my_retain(retain_ref)
    here = lax.div(lax.axis_index("wide"), PLANE)
    ahead, ahead_tail, back, back_tail = plane_ends(blocks_ref, retain)
    reflect = power(retain, 33) * beyond_here(planes, here, retain)
    back = back - reflect * ahead
    back_tail = back_tail - reflect * ahead_tail
    for q in range(planes):
        out_ref[slot_z(q, planes), :, :128] = jnp.where(q > here, ahead, back)
        out_ref[slot_z(q, planes), :, 128:] = jnp.where(q > here, ahead_tail, back_tail)


def across_in(planes, blocks_ref, others_ref, retain_ref, out_ref):
    retain = my_retain(retain_ref)
    here = lax.div(lax.axis_index("wide"), PLANE)
    ahead, ahead_tail, _, _ = plane_ends(blocks_ref, retain)
    four, plane = power(retain, 4), power(retain, 32)
    reflect = retain * beyond_here(planes, here, retain)
    enter, leave = [0.0, 0.0], [0.0, 0.0]
    for q in range(planes):
        back = planes - 1 - q
        for part in range(2):
            at = slice(128 * part, 128 * part + 128)
            enter[part] = jnp.where(q < here, plane * enter[part] + others_ref[slot_z(q, planes), :, at], enter[part])
            leave[part] = jnp.where(back > here, plane * leave[part] + others_ref[slot_z(back, planes), :, at], leave[part])
    leave[0] = leave[0] - reflect * (ahead + plane * enter[0])
    leave[1] = leave[1] - reflect * (ahead_tail + plane * enter[1])
    left = lanes((8, 128)) < 64
    leave[1] = pltpu.roll(leave[1], 64, 1)
    tails = []
    for m in range(PLANE):
        out_ref[slot_m(m), :, :128] = enter[0]
        tails.append(enter[1])
        enter[0] = four * enter[0] + blocks_ref[slot_m(m), :, :128]
        enter[1] = four * enter[1] + blocks_ref[slot_m(m), :, 256:]
    for m in reversed(range(PLANE)):
        out_ref[slot_m(m), :, 128:256] = leave[0]
        out_ref[slot_m(m), :, 256:] = jnp.where(left, tails[m], leave[1])
        leave[0] = four * leave[0] + blocks_ref[slot_m(m), :, 128:256]
        leave[1] = four * leave[1] + blocks_ref[slot_m(m), :, 256:]


def after_scan(
    got_ref, own_ref, left_ref, right_ref, y_second_ref, y_first_ref, u2_ref, both_ref, deep_first_ref, deep_second_ref, smooth_ref, vert_ref, retain_ref, weight_ref,
    pressure_ref, residual_ref, tails_ref, coarse_ref, line, corr, ua, ub,
):
    even = lax.rem(lax.axis_index("wide"), 2) == 0
    left_rows, left_coarse = unpack_deep(lambda i: jnp.where(even, deep_second_ref[i], deep_first_ref[i]))
    right_rows, right_coarse = unpack_deep(lambda i: jnp.where(even, deep_first_ref[i], deep_second_ref[i]))
    for j in range(2):
        coarse_ref[j] = left_coarse[j]
        coarse_ref[6 + j] = right_coarse[j]
    for j in range(2):
        coarse_ref[2 + 2 * j], coarse_ref[3 + 2 * j] = unfold(both_ref[j])
    low, high = y_sides(y_first_ref, y_second_ref)
    for r in range(NR):
        tails_ref[r] = beyond(low, high, r)
    retain, weight = wide3(retain_ref[...]), wide3(weight_ref[...])
    inv_retain = 1.0 / retain
    coarse_lane = lax.broadcasted_iota(jnp.int32, (256, LX), 0)
    fine_lane = lax.broadcasted_iota(jnp.int32, (256, LX), 1)
    spread = jnp.where(fine_lane // 2 == coarse_lane, 1.0, 0.0)
    keep_left = lanes((K, 128)) < 64
    tail = got_ref[:, 256:]
    both = jnp.concatenate(
        [
            jnp.concatenate([got_ref[:, :128], jnp.where(keep_left, tail, 0.0)], axis=1),
            jnp.concatenate([got_ref[:, 128:256], jnp.where(keep_left, pltpu.roll(tail, 64, 1), 0.0)], axis=1),
        ],
        axis=0,
    )
    both = select(both, spread)

    def row(r, levels=K):
        return whole_row(own_ref, left_ref, right_ref, tails_ref, r, levels)

    def coef(j):
        if j == 0:
            pair = row(0, K + 1)[1] + row(1, K + 1)[1]
        elif j == 7:
            pair = row(NR - 2, K + 1)[1] + row(NR - 1, K + 1)[1]
        else:
            pair = row(2 * j + HX - 4)[1] + row(2 * j + HX - 3)[1]
        return 0.0625 * pair_sum(pair)

    coefs = [coef(j) for j in range(8)]
    enter, leave = both[:K], both[K:]
    reach = leave
    for j in (4, 5):
        reach = (reach - coarse_ref[j + 2]) * inv_retain
        line[j + 1 + 3] = reach
    reach = leave
    line[4 + 3] = reach
    for j in (3, 2, 1, 0, -1, -2):
        reach = coarse_ref[j + 2] + retain * reach
        line[j + 3] = reach
    ahead = (enter - coarse_ref[1]) * inv_retain
    ahead = (ahead - coarse_ref[0]) * inv_retain
    line[0] = jnp.where(coefs[0] > 0.0, weight * (ahead + retain * line[1]), 0.0)
    for j in range(-2, 7):
        inside = coefs[min(max(j + 2, 0), 7)] > 0.0
        start = retain * ahead
        line[j + 3] = jnp.where(inside, weight * (start + line[j + 3]), 0.0)
        if j < 6:
            ahead = enter if j == -1 else coarse_ref[j + 2] + start

    smooth = smooth_ref[...]

    for j in range(8):
        v = line[j + 1]
        term = smooth_term(v, coarse_ref[j], coefs[j], line[j], line[j + 2], 2, 4.0)
        corr[j] = 0.6 * v + apply3(smooth, term)
    for i in range(14):
        field = left_rows[i] if i < 2 else right_rows[i - 12] if i >= 12 else u2_ref[i - 2]
        ua[i] = field + corr[(i - 3) // 2 + 2]

    for source, target, least, most in ((ua, ub, 1, 13), (ub, ua, 2, 12)):
        for i in range(least, most):
            u, (rhs, area) = source[i], row(i + HX - 3)
            term = smooth_term(u, rhs, area, source[i - 1], source[i + 1], 1, 4.0)
            target[i] = 0.6 * u + apply3(smooth, term)
    vert = vert_ref[...]
    for x in range(8):
        i = x + 3
        u = ua[i]
        rhs, area = row(x + HX)
        term = smooth_term(u, rhs, area, ua[i - 1], ua[i + 1], 1)
        rest = term[:, :256] - apply3(vert, u[:, :256])
        for t in range(2):
            here = pl.ds(8 * t + x, K, stride=16)
            pressure_ref[here, :] = u[:, 128 * t : 128 * t + 128]
            residual_ref[here, :] = rest[:, 128 * t : 128 * t + 128]


def local(rhs, areas, stiffness):
    wide, narrow = lax.axis_size("wide"), lax.axis_size("narrow")
    planes = wide // PLANE
    rhs = rhs.reshape(K, 8, 2, 128).transpose(0, 2, 1, 3).reshape(K * 16, 128)
    up, down, own = call(
        pack_x,
        [((HX, KA, 256), f32)] * 2 + [((8, KA, 256), f32)],
        [pltpu.VMEM((K * 16, 128), f32), pltpu.VMEM((8, 256), f32), pltpu.SemaphoreType.DMA((2,))],
        [pl.BlockSpec(memory_space=pltpu.HBM)] * 2,
    )(*(pltpu.with_memory_space_constraint(x, pltpu.HBM) for x in (rhs, areas)))

    def in_pairs(first, second, axis, count):
        second = lax.ppermute(second, axis, [(i, ((i + 1) ^ 1) - 1) for i in range(1, count - 1)])
        return lax.ppermute(first, axis, [(i, i ^ 1) for i in range(count)]), second

    x_first, x_second = in_pairs(up, down, "wide", wide)
    smooth, vert, retain, weight = call(
        tables,
        [((K, 192), bf16)] * 2 + [((K, 128), f32)] * 2,
        [pltpu.VMEM((K, 128), f32)] * 2,
        [pl.BlockSpec(memory_space=pltpu.SMEM)],
    )(stiffness)
    first, second, left, right = call(
        pack_y, [((KA, 128), f32)] * 2 + [((HX, KA, 256), f32)] * 2, specs=on_vmem(4)
    )(own, x_first, x_second, retain)
    first, second = in_pairs(first, second, "narrow", narrow)
    (u1,) = call(first_main, [((NR, K, 256), f32)], specs=on_vmem(4))(own, left, right, smooth)
    sent, u2, coarse = call(
        before_scan,
        K2_OUTS,
        K2_SCRATCH,
        on_vmem(9),
    )(own, left, right, second, first, u1, smooth, vert, retain)
    in_plane = [[p * PLANE + (s + FIRST_M) % PLANE for s in range(PLANE)] for p in range(planes)]
    over_planes = [[(s + FIRST_Z) % planes * PLANE + m for s in range(planes)] for m in range(PLANE)]

    def exchange(array, groups):
        return lax.all_to_all(array, "wide", 0, 0, tiled=True, axis_index_groups=groups)

    blocks = exchange(sent.reshape(PLANE, 8, LX), in_plane)
    blocks, u2, coarse = lax.optimization_barrier((blocks, u2, coarse))
    deep_first, deep_second = call(pack_deep, [((7, K, 128), f32)] * 2, specs=on_vmem(2))(u2, coarse)
    deep_first, deep_second = in_pairs(deep_first, deep_second, "wide", wide)
    (out,) = call(functools.partial(across_out, planes), [((planes, 8, 256), f32)], specs=on_vmem(2))(blocks, retain)
    others = exchange(out, over_planes)
    (back,) = call(functools.partial(across_in, planes), [((PLANE, 8, LX), f32)], specs=on_vmem(3))(
        blocks, others, retain
    )
    got = exchange(back, in_plane).reshape(K, LX)
    pressure, residual = call(
        after_scan,
        [((K * 16, 128), f32)] * 2,
        K4_SCRATCH,
        on_vmem(14),
    )(got, own, left, right, second, first, u2, coarse, deep_first, deep_second, smooth, vert, retain, weight)
    return tuple(
        out.reshape(K, 2, 8, 128).transpose(0, 2, 1, 3).reshape(K, 8, 256) for out in (pressure, residual)
    )


def solution(mesh):
    placed = (P(None, "wide", "narrow"), P("wide", "narrow"), P())
    return jax.shard_map(
        local,
        mesh=mesh,
        in_specs=placed,
        out_specs=(P(None, "wide", "narrow"), P(None, "wide", "narrow")),
        check_vma=False,
    )
```

```python
import functools

import jax
import jax.numpy as jnp
from jax import lax
from jax.experimental import pallas as pl
from jax.experimental.pallas import tpu as pltpu
from jax.sharding import PartitionSpec as P

K = 64
KA = 72
HX = 2
HY = 8
NR = 8 + 2 * HX
LX = 384
PLANE = 8
FIRST_M = 4
FIRST_Z = 10
f32, bf16 = jnp.float32, jnp.bfloat16
K2_OUTS = [((K, LX), f32), ((10, K, LX), f32), ((2, K, LX), f32)]
K2_SCRATCH = [pltpu.VMEM(s, f32) for s in ((NR, KA, 128), (NR, K, LX), (4, K, LX), (NR, K, 128))]
K4_SCRATCH = [
    pltpu.VMEM(s, f32)
    for s in ((NR, KA, 128), (8, K, LX), (10, K, LX), (8, K, LX), (14, K, LX), (14, K, LX))
]
LIMIT = 16 * 1024 * 1024


def call(kernel, outs, scratch=(), specs=None):
    vmem = pl.BlockSpec(memory_space=pltpu.VMEM)
    return pl.pallas_call(
        kernel,
        out_shape=[jax.ShapeDtypeStruct(s, d) for s, d in outs],
        in_specs=specs,
        out_specs=[vmem] * len(outs),
        scratch_shapes=list(scratch),
        compiler_params=pltpu.CompilerParams(vmem_limit_bytes=LIMIT),
    )


def on_vmem(n):
    return [pl.BlockSpec(memory_space=pltpu.VMEM)] * n


def lanes(shape):
    return lax.broadcasted_iota(jnp.int32, shape, len(shape) - 1)


def wide3(table):
    return jnp.concatenate([table] * (LX // 128), axis=1)


def apply3(cat, x):
    high = x.astype(bf16)
    low = (x - high.astype(f32)).astype(bf16)
    return jnp.dot(cat, jnp.concatenate([high, high, low], axis=0), preferred_element_type=f32)


def select(x, picks):
    high = x.astype(bf16)
    rest = x - high.astype(f32)
    middle = rest.astype(bf16)
    low = (rest - middle.astype(f32)).astype(bf16)
    rows = x.shape[0]
    parts = jnp.dot(jnp.concatenate([high, middle, low], axis=0), picks.astype(bf16), preferred_element_type=f32)
    return parts[:rows] + (parts[rows : 2 * rows] + parts[2 * rows :])


def split3(matrix):
    high = matrix.astype(bf16)
    low = (matrix - high.astype(f32)).astype(bf16)
    return jnp.concatenate([high, low, high], axis=1)


def pack_x(rhs_hbm, areas_hbm, first_ref, second_ref, own_ref, rhs, areas, sems):
    copies = [
        pltpu.make_async_copy(rhs_hbm, rhs, sems.at[0]),
        pltpu.make_async_copy(areas_hbm, areas, sems.at[1]),
    ]
    for copy in copies:
        copy.start()
    for copy in copies:
        copy.wait()
    first = lax.broadcasted_iota(jnp.int32, (KA - K, 256), 0) == 0

    def area(x, beyond):
        return jnp.where(first, areas[x : x + 1, :], areas[beyond : beyond + 1, :])

    for x in range(8):
        for t in range(2):
            own_ref[x, :K, 128 * t : 128 * t + 128] = rhs[pl.ds(8 * t + x, K, stride=16), :]
        own_ref[x, K:, :] = area(x, x)
    even = lax.rem(lax.axis_index("wide"), 2) == 0
    for x in range(HX):
        up, down = own_ref[8 - HX + x, :K, :], own_ref[x, :K, :]
        up_area, down_area = area(8 - HX + x, 8 - 2 * HX + x), area(x, x + HX)
        first_ref[x, :K, :] = jnp.where(even, up, down)
        first_ref[x, K:, :] = jnp.where(even, up_area, down_area)
        second_ref[x, :K, :] = jnp.where(even, down, up)
        second_ref[x, K:, :] = jnp.where(even, down_area, up_area)


def tables(stiff_ref, smooth_ref, vert_ref, retain_ref, weight_ref, lead, trail):
    scale = 7.5
    row = lax.broadcasted_iota(jnp.int32, (K, 128), 0)
    col = lax.broadcasted_iota(jnp.int32, (K, 128), 1)
    lane = lanes((1, 128))
    one = jnp.ones((1, 128), f32)
    zero = jnp.zeros((1, 128), f32)
    before, now, lead_row = zero, one, zero
    after, later, trail_row = zero, one, zero
    for k in range(K):
        lead[pl.ds(k, 1), :] = now
        lead_row = jnp.where(lane == k, now, lead_row)
        now, before = (stiff_ref[k] + 8.0) * (1.0 / scale) * now - (4.0 / scale**2) * before, now
        at = K - 1 - k
        trail[pl.ds(at, 1), :] = later
        trail_row = jnp.where(lane == at, later, trail_row)
        later, after = (stiff_ref[at] + 8.0) * (1.0 / scale) * later - (4.0 / scale**2) * after, later
    gap = jnp.abs(row - col)
    decay = jnp.ones((K, 128), f32)
    for b in range(6):
        decay = decay * jnp.where((gap >> b) & 1 == 1, (2.0 / scale) ** (1 << b), 1.0)
    upper = lead[...] * trail_row
    lower = lead_row * trail[...]
    inverse = decay * jnp.where(row <= col, upper, lower) / (scale * now)
    smooth_ref[...] = split3((0.4 * inverse)[:, :K])
    stiff_row = zero
    for k in range(K):
        stiff_row = jnp.where(lane == k, stiff_ref[k], stiff_row)
    diagonal = jnp.where(row == col, stiff_row, 0.0)
    stiff = jnp.broadcast_to(jnp.sum(diagonal, axis=1, keepdims=True), (K, 128))
    vert = jnp.where(row == col, stiff + 4.0, jnp.where(gap == 1, -2.0, 0.0))
    vert_ref[...] = split3(vert[:, :K])
    keep = jnp.sqrt(stiff + 0.25 * stiff * stiff) - 0.5 * stiff
    retain_ref[...] = 1.0 - keep
    weight_ref[...] = keep / (2.0 - keep)


def ext_row(own_ref, left_ref, right_ref, r):
    if r < HX:
        return left_ref[r]
    if r >= HX + 8:
        return right_ref[r - HX - 8]
    return own_ref[r - HX]


def whole_row(own_ref, left_ref, right_ref, tails_ref, r, levels=K):
    main = ext_row(own_ref, left_ref, right_ref, r)
    tail = tails_ref[r]
    at = slice(levels, levels + 1)
    return (
        jnp.concatenate([main[:K], tail[:K]], axis=1),
        jnp.concatenate([main[at], tail[at]], axis=1),
    )


def pack_y(own_ref, x_first_ref, x_second_ref, _, first_ref, second_ref, left_ref, right_ref):
    even = lax.rem(lax.axis_index("wide"), 2) == 0
    left_ref[...] = jnp.where(even, x_second_ref[...], x_first_ref[...])
    right_ref[...] = jnp.where(even, x_first_ref[...], x_second_ref[...])
    lane = lanes((KA, 128))
    low = high = jnp.zeros((KA, 128), f32)
    for r in range(NR):
        row = ext_row(own_ref, left_ref, right_ref, r)
        o = HY * r
        here = (lane >= o) & (lane < o + HY)
        low = jnp.where(here, pltpu.roll(row[:, :128], o, 1), low)
        high = jnp.where(here, pltpu.roll(row[:, 128:], o + HY, 1), high)
    even = lax.rem(lax.axis_index("narrow"), 2) == 0
    first_ref[...] = jnp.where(even, high, low)
    second_ref[...] = jnp.where(even, low, high)


def first_main(own_ref, left_ref, right_ref, smooth_ref, u1_ref):
    smooth = smooth_ref[...]
    for r in range(NR):
        u1_ref[r] = apply3(smooth, ext_row(own_ref, left_ref, right_ref, r)[:K])


def smooth_term(u, rhs, area, above, below, step, more=0.0):
    beside = above + below + pltpu.roll(u, step, 1) + pltpu.roll(u, LX - step, 1)
    return rhs + ((more - 4.0 * area) * u + area * beside)


def pair_sum(v):
    even = lanes(v.shape) % 2 == 0
    return v + jnp.where(even, pltpu.roll(v, LX - 1, 1), pltpu.roll(v, 1, 1))


def y_sides(first_ref, second_ref):
    even = lax.rem(lax.axis_index("narrow"), 2) == 0
    first, second = first_ref[...], second_ref[...]
    return jnp.where(even, first, second), jnp.where(even, second, first)


def beyond(right, left, r):
    lane = lanes(right.shape)
    right = pltpu.roll(right, (128 - HY * r) % 128, 1)
    left = pltpu.roll(left, 128 - HY - HY * r, 1)
    return jnp.where(lane < HY, right, jnp.where(lane >= 128 - HY, left, 0.0))


def pack_deep(u2_ref, both_ref, first_ref, second_ref):
    lane = lanes((K, 128))
    even = lax.rem(lax.axis_index("wide"), 2) == 0
    tails = [jnp.zeros((K, 128), f32)] * 2
    for i in range(3):
        if i < 2:
            sides = u2_ref[6 + i], u2_ref[2 + i]
        else:
            sides = both_ref[1], both_ref[0]
        here = (lane >= 16 * i) & (lane < 16 * i + 16)
        rows = jnp.where(even, sides[0], sides[1]), jnp.where(even, sides[1], sides[0])
        for n, ref in enumerate((first_ref, second_ref)):
            ref[2 * i] = rows[n][:, :128]
            ref[2 * i + 1] = rows[n][:, 128:256]
            tails[n] = jnp.where(here, pltpu.roll(rows[n][:, 256:], HY + 16 * i, 1), tails[n])
    first_ref[6] = tails[0]
    second_ref[6] = tails[1]


def unpack_deep(got):
    lane = lanes((K, 128))
    edge = (lane < HY) | (lane >= 128 - HY)
    rows = []
    for i in range(3):
        tail = jnp.where(edge, pltpu.roll(got(6), 128 - HY - 16 * i, 1), 0.0)
        rows.append(jnp.concatenate([got(2 * i), got(2 * i + 1), tail], axis=1))
    return rows, unfold(rows.pop())


def unfold(both):
    even = lanes((K, LX)) % 2 == 0
    first = jnp.where(even, both, pltpu.roll(both, 1, 1))
    second = jnp.where(even, pltpu.roll(both, LX - 1, 1), both)
    return first, second


def before_scan(
    own_ref, left_ref, right_ref, first_ref, second_ref, u1_ref, smooth_ref, vert_ref, retain_ref,
    sent_ref, u2_ref, both_ref, tails_ref, fine, coarse_ref, u1,
):
    smooth = smooth_ref[...]
    low, high = y_sides(first_ref, second_ref)
    tails = apply3(smooth, jnp.concatenate([low[:K], high[:K]], axis=1))

    for r in range(NR):
        tails_ref[r] = beyond(low, high, r)
        u1[r] = beyond(tails[:, :128], tails[:, 128:], r)

    def row(r):
        return whole_row(own_ref, left_ref, right_ref, tails_ref, r)

    def first(r):
        return jnp.concatenate([u1_ref[r], u1[r]], axis=1)

    for r in range(1, NR - 1):
        u, (rhs, area) = first(r), row(r)
        term = smooth_term(u, rhs, area, first(r - 1), first(r + 1), 1, 4.0)
        fine[r] = 0.6 * u + apply3(smooth, term)
    vert = vert_ref[...]
    for j in range(4):
        total, field = 0.0, 0.0
        for at in (2 * j + HX, 2 * j + HX + 1):
            u, (rhs, area) = fine[at], row(at)
            total += smooth_term(u, rhs, area, fine[at - 1], fine[at + 1], 1)
            field += u
        coarse_ref[j] = 0.25 * (pair_sum(total) - apply3(vert, pair_sum(field)))
    for x in range(10):
        u2_ref[x] = fine[x + 1]
    parity = lanes((K, LX)) % 2 == 0
    for j in range(2):
        both_ref[j] = jnp.where(parity, coarse_ref[2 * j], coarse_ref[2 * j + 1])
    retain = wide3(retain_ref[...])
    ahead = coarse_ref[0]
    back = coarse_ref[3]
    for j in range(1, 4):
        ahead = retain * ahead + coarse_ref[j]
        back = retain * back + coarse_ref[3 - j]
    fine_lane = lax.broadcasted_iota(jnp.int32, (LX, 256), 0)
    coarse_lane = lax.broadcasted_iota(jnp.int32, (LX, 256), 1)
    pick = jnp.where(fine_lane == 2 * coarse_lane, 1.0, 0.0)
    both = select(jnp.concatenate([ahead, back], axis=0), pick)
    sent_ref[:, :128] = both[:K, :128]
    sent_ref[:, 128:256] = both[K:, :128]
    sent_ref[:, 256:] = both[:K, 128:] + pltpu.roll(both[K:, 128:], 64, 1)


def power(x, n):
    out = None
    while n:
        if n & 1:
            out = x if out is None else out * x
        x = x * x
        n >>= 1
    return out


def my_retain(retain_ref):
    at = lax.rem(lax.axis_index("wide") + PLANE - FIRST_M, PLANE)
    return retain_ref[pl.ds(pl.multiple_of(at * 8, 8), 8), :]


def beyond_here(planes, here, retain):
    left, step = planes - 1 - here, power(retain, 64)
    out = jnp.ones_like(retain)
    for b in range((planes - 1).bit_length()):
        out = jnp.where((left >> b) & 1 == 1, out * step, out)
        step = step * step
    return out


def slot_m(m):
    return (m - FIRST_M) % PLANE


def slot_z(q, planes):
    return (q - FIRST_Z) % planes


def plane_ends(blocks, retain):
    four = power(retain, 4)
    ends = []
    for order, part in ((range(PLANE), 0), (reversed(range(PLANE)), 1)):
        main, tail = 0.0, 0.0
        for m in order:
            main = four * main + blocks[slot_m(m), :, 128 * part : 128 * part + 128]
            tail = four * tail + blocks[slot_m(m), :, 256:]
        ends += [main, tail if part == 0 else pltpu.roll(tail, 64, 1)]
    return ends


def across_out(planes, blocks_ref, retain_ref, out_ref):
    retain = my_retain(retain_ref)
    here = lax.div(lax.axis_index("wide"), PLANE)
    ahead, ahead_tail, back, back_tail = plane_ends(blocks_ref, retain)
    reflect = power(retain, 33) * beyond_here(planes, here, retain)
    back = back - reflect * ahead
    back_tail = back_tail - reflect * ahead_tail
    for q in range(planes):
        out_ref[slot_z(q, planes), :, :128] = jnp.where(q > here, ahead, back)
        out_ref[slot_z(q, planes), :, 128:] = jnp.where(q > here, ahead_tail, back_tail)


def across_in(planes, blocks_ref, others_ref, retain_ref, out_ref):
    retain = my_retain(retain_ref)
    here = lax.div(lax.axis_index("wide"), PLANE)
    ahead, ahead_tail, _, _ = plane_ends(blocks_ref, retain)
    four, plane = power(retain, 4), power(retain, 32)
    reflect = retain * beyond_here(planes, here, retain)
    enter, leave = [0.0, 0.0], [0.0, 0.0]
    for q in range(planes):
        back = planes - 1 - q
        for part in range(2):
            at = slice(128 * part, 128 * part + 128)
            enter[part] = jnp.where(q < here, plane * enter[part] + others_ref[slot_z(q, planes), :, at], enter[part])
            leave[part] = jnp.where(back > here, plane * leave[part] + others_ref[slot_z(back, planes), :, at], leave[part])
    leave[0] = leave[0] - reflect * (ahead + plane * enter[0])
    leave[1] = leave[1] - reflect * (ahead_tail + plane * enter[1])
    left = lanes((8, 128)) < 64
    leave[1] = pltpu.roll(leave[1], 64, 1)
    tails = []
    for m in range(PLANE):
        out_ref[slot_m(m), :, :128] = enter[0]
        tails.append(enter[1])
        enter[0] = four * enter[0] + blocks_ref[slot_m(m), :, :128]
        enter[1] = four * enter[1] + blocks_ref[slot_m(m), :, 256:]
    for m in reversed(range(PLANE)):
        out_ref[slot_m(m), :, 128:256] = leave[0]
        out_ref[slot_m(m), :, 256:] = jnp.where(left, tails[m], leave[1])
        leave[0] = four * leave[0] + blocks_ref[slot_m(m), :, 128:256]
        leave[1] = four * leave[1] + blocks_ref[slot_m(m), :, 256:]


def after_scan(
    got_ref, own_ref, left_ref, right_ref, y_second_ref, y_first_ref, u2_ref, both_ref, deep_first_ref, deep_second_ref, smooth_ref, vert_ref, retain_ref, weight_ref,
    pressure_ref, residual_ref, tails_ref, coarse_ref, line, corr, ua, ub,
):
    even = lax.rem(lax.axis_index("wide"), 2) == 0
    left_rows, left_coarse = unpack_deep(lambda i: jnp.where(even, deep_second_ref[i], deep_first_ref[i]))
    right_rows, right_coarse = unpack_deep(lambda i: jnp.where(even, deep_first_ref[i], deep_second_ref[i]))
    for j in range(2):
        coarse_ref[j] = left_coarse[j]
        coarse_ref[6 + j] = right_coarse[j]
    for j in range(2):
        coarse_ref[2 + 2 * j], coarse_ref[3 + 2 * j] = unfold(both_ref[j])
    low, high = y_sides(y_first_ref, y_second_ref)
    for r in range(NR):
        tails_ref[r] = beyond(low, high, r)
    retain, weight = wide3(retain_ref[...]), wide3(weight_ref[...])
    inv_retain = 1.0 / retain
    coarse_lane = lax.broadcasted_iota(jnp.int32, (256, LX), 0)
    fine_lane = lax.broadcasted_iota(jnp.int32, (256, LX), 1)
    spread = jnp.where(fine_lane // 2 == coarse_lane, 1.0, 0.0)
    keep_left = lanes((K, 128)) < 64
    tail = got_ref[:, 256:]
    both = jnp.concatenate(
        [
            jnp.concatenate([got_ref[:, :128], jnp.where(keep_left, tail, 0.0)], axis=1),
            jnp.concatenate([got_ref[:, 128:256], jnp.where(keep_left, pltpu.roll(tail, 64, 1), 0.0)], axis=1),
        ],
        axis=0,
    )
    both = select(both, spread)

    def row(r, levels=K):
        return whole_row(own_ref, left_ref, right_ref, tails_ref, r, levels)

    def coef(j):
        if j == 0:
            pair = row(0, K + 1)[1] + row(1, K + 1)[1]
        elif j == 7:
            pair = row(NR - 2, K + 1)[1] + row(NR - 1, K + 1)[1]
        else:
            pair = row(2 * j + HX - 4)[1] + row(2 * j + HX - 3)[1]
        return 0.0625 * pair_sum(pair)

    coefs = [coef(j) for j in range(8)]
    enter, leave = both[:K], both[K:]
    reach = leave
    for j in (4, 5):
        reach = (reach - coarse_ref[j + 2]) * inv_retain
        line[j + 1 + 3] = reach
    reach = leave
    line[4 + 3] = reach
    for j in (3, 2, 1, 0, -1, -2):
        reach = coarse_ref[j + 2] + retain * reach
        line[j + 3] = reach
    ahead = (enter - coarse_ref[1]) * inv_retain
    ahead = (ahead - coarse_ref[0]) * inv_retain
    line[0] = jnp.where(coefs[0] > 0.0, weight * (ahead + retain * line[1]), 0.0)
    for j in range(-2, 7):
        inside = coefs[min(max(j + 2, 0), 7)] > 0.0
        start = retain * ahead
        line[j + 3] = jnp.where(inside, weight * (start + line[j + 3]), 0.0)
        if j < 6:
            ahead = enter if j == -1 else coarse_ref[j + 2] + start

    smooth = smooth_ref[...]

    for j in range(8):
        v = line[j + 1]
        term = smooth_term(v, coarse_ref[j], coefs[j], line[j], line[j + 2], 2, 4.0)
        corr[j] = 0.6 * v + apply3(smooth, term)
    for i in range(14):
        field = left_rows[i] if i < 2 else right_rows[i - 12] if i >= 12 else u2_ref[i - 2]
        ua[i] = field + corr[(i - 3) // 2 + 2]

    for source, target, least, most in ((ua, ub, 1, 13), (ub, ua, 2, 12)):
        for i in range(least, most):
            u, (rhs, area) = source[i], row(i + HX - 3)
            term = smooth_term(u, rhs, area, source[i - 1], source[i + 1], 1, 4.0)
            target[i] = 0.6 * u + apply3(smooth, term)
    vert = vert_ref[...]
    for x in range(8):
        i = x + 3
        u = ua[i]
        rhs, area = row(x + HX)
        term = smooth_term(u, rhs, area, ua[i - 1], ua[i + 1], 1)
        rest = term[:, :256] - apply3(vert, u[:, :256])
        for t in range(2):
            here = pl.ds(8 * t + x, K, stride=16)
            pressure_ref[here, :] = u[:, 128 * t : 128 * t + 128]
            residual_ref[here, :] = rest[:, 128 * t : 128 * t + 128]


def local(rhs, areas, stiffness):
    wide, narrow = lax.axis_size("wide"), lax.axis_size("narrow")
    planes = wide // PLANE
    rhs = rhs.reshape(K, 8, 2, 128).transpose(0, 2, 1, 3).reshape(K * 16, 128)
    up, down, own = call(
        pack_x,
        [((HX, KA, 256), f32)] * 2 + [((8, KA, 256), f32)],
        [pltpu.VMEM((K * 16, 128), f32), pltpu.VMEM((8, 256), f32), pltpu.SemaphoreType.DMA((2,))],
        [pl.BlockSpec(memory_space=pltpu.HBM)] * 2,
    )(*(pltpu.with_memory_space_constraint(x, pltpu.HBM) for x in (rhs, areas)))

    def in_pairs(first, second, axis, count):
        second = lax.ppermute(second, axis, [(i, ((i + 1) ^ 1) - 1) for i in range(1, count - 1)])
        return lax.ppermute(first, axis, [(i, i ^ 1) for i in range(count)]), second

    x_first, x_second = in_pairs(up, down, "wide", wide)
    smooth, vert, retain, weight = call(
        tables,
        [((K, 192), bf16)] * 2 + [((K, 128), f32)] * 2,
        [pltpu.VMEM((K, 128), f32)] * 2,
        [pl.BlockSpec(memory_space=pltpu.SMEM)],
    )(stiffness)
    first, second, left, right = call(
        pack_y, [((KA, 128), f32)] * 2 + [((HX, KA, 256), f32)] * 2, specs=on_vmem(4)
    )(own, x_first, x_second, retain)
    first, second = in_pairs(first, second, "narrow", narrow)
    (u1,) = call(first_main, [((NR, K, 256), f32)], specs=on_vmem(4))(own, left, right, smooth)
    sent, u2, coarse = call(
        before_scan,
        K2_OUTS,
        K2_SCRATCH,
        on_vmem(9),
    )(own, left, right, first, second, u1, smooth, vert, retain)
    in_plane = [[p * PLANE + (s + FIRST_M) % PLANE for s in range(PLANE)] for p in range(planes)]
    over_planes = [[(s + FIRST_Z) % planes * PLANE + m for s in range(planes)] for m in range(PLANE)]

    def exchange(array, groups):
        return lax.all_to_all(array, "wide", 0, 0, tiled=True, axis_index_groups=groups)

    blocks = exchange(sent.reshape(PLANE, 8, LX), in_plane)
    blocks, u2, coarse = lax.optimization_barrier((blocks, u2, coarse))
    deep_first, deep_second = call(pack_deep, [((7, K, 128), f32)] * 2, specs=on_vmem(2))(u2, coarse)
    deep_first, deep_second = in_pairs(deep_first, deep_second, "wide", wide)
    (out,) = call(functools.partial(across_out, planes), [((planes, 8, 256), f32)], specs=on_vmem(2))(blocks, retain)
    others = exchange(out, over_planes)
    (back,) = call(functools.partial(across_in, planes), [((PLANE, 8, LX), f32)], specs=on_vmem(3))(
        blocks, others, retain
    )
    got = exchange(back, in_plane).reshape(K, LX)
    pressure, residual = call(
        after_scan,
        [((K * 16, 128), f32)] * 2,
        K4_SCRATCH,
        on_vmem(14),
    )(got, own, left, right, second, first, u2, coarse, deep_first, deep_second, smooth, vert, retain, weight)
    return tuple(
        out.reshape(K, 2, 8, 128).transpose(0, 2, 1, 3).reshape(K, 8, 256) for out in (pressure, residual)
    )


def solution(mesh):
    placed = (P(None, "wide", "narrow"), P("wide", "narrow"), P())
    return jax.shard_map(
        local,
        mesh=mesh,
        in_specs=placed,
        out_specs=(P(None, "wide", "narrow"), P(None, "wide", "narrow")),
        check_vma=False,
    )
```
